512 devices in a mesh: region: 8 (over y_lo, core), space: 64 (over y_hi, x, z).
Axes of the slice: x: 4, y: 8 (y_hi: 2, y_lo: 4; y = y_hi * 4 + y_lo), z: 8, core: 2. Of those that a mesh axis runs over, the one named last changes fastest.
Arguments:
- tokens: bfloat16 [8, 18432, 384], P('region', 'space'), may hold values from -6 to 6
- cotangent: bfloat16 [8, 18432, 384], P('region', 'space'), may hold values from -6 to 6
- neighbours: int32 [8, 576, 27], P('region', 'space'), may hold values from -1 to 575, as said below
- active: int32 [8, 576], P('region', 'space'), may hold values from 0 to 1
- gain: float32 [384], replicated, may hold values from 0.1 to 1.9
- w_qkv: bfloat16 [384, 1152], replicated, may hold values from -4.082483 to 4.082483
- w_out: bfloat16 [384, 384], replicated, may hold values from -0.3125 to 0.3125
Outputs:
- grad_input: bfloat16 [8, 18432, 384], P('region', 'space')
- grad_qkv: float32 [384, 1152], replicated
- grad_out: float32 [384, 384], replicated
- grad_gain: float32 [384], replicated
The draws below stay inside these ranges and needn't reach their ends.
Inputs may be any that keep to these rules, and one draw needn't show every extreme that they name: `neighbours`: row b lists first b itself, then the other active blocks of its region whose layer, row and column each differ from b's by at most one, each once; the rest is -1, and the row of an inactive block is all -1. In every region some block lists 27 blocks.
All inputs are finite; a program needn't handle non-finite values.
Results may differ from the reference program's by a relative error of at most 0.012.
Values may be sent and summed in bfloat16 or wider, within the bound.
No kernel may reach another device: no remote copies, remote signals or barrier semaphores. Data moves between devices by JAX's collectives and lax.ppermute only.
A program may use at most 64 MiB of HBM per device.

```python
import jax
import jax.numpy as jnp
import numpy as np
from jax import lax

D = 384
HEADS = 6
BT = 32
NBR = 27
GY = 3
GZ = 3
BPD = 9
SLAB_TOKENS = 288
NBLK = 576
TOK_REGION = 18432
REGIONS = 8


def structure(key):
    side = GY * GZ
    layer_count = NBLK // side
    first, second, third = jax.random.split(key, 3)
    density = jax.random.randint(first, (REGIONS, layer_count, 1), 2, 11)
    rolls = jax.random.randint(second, (REGIONS, layer_count, side), 0, 10)
    centre = jax.random.randint(third, (REGIONS, 1), 1, layer_count - 1)
    layer_ids = jnp.arange(layer_count)[None, :]
    forced = jnp.abs(layer_ids - centre) <= 1
    alive = (rolls < density) | forced[:, :, None]
    alive = alive.reshape(REGIONS, NBLK).astype(jnp.int32)
    table = [[0, 0, 0]]
    for step_x in (-1, 0, 1):
        for step_y in (-1, 0, 1):
            for step_z in (-1, 0, 1):
                if step_x != 0 or step_y != 0 or step_z != 0:
                    table.append([step_x, step_y, step_z])
    offsets = np.array(table, dtype=np.int32)
    blocks = jnp.arange(NBLK, dtype=jnp.int32)
    layer_of = blocks // side
    row_of = blocks // GZ % GY
    col_of = blocks % GZ
    next_layer = layer_of[:, None] + offsets[None, :, 0]
    next_row = row_of[:, None] + offsets[None, :, 1]
    next_col = col_of[:, None] + offsets[None, :, 2]
    inside = (next_layer >= 0) & (next_layer < layer_count) & (next_row >= 0) & (next_row < GY) & (next_col >= 0) & (next_col < GZ)
    candidate = jnp.where(inside, (next_layer * GY + next_row) * GZ + next_col, 0).astype(jnp.int32)
    valid = inside[None, :, :] & (alive[:, candidate] == 1) & (alive[:, :, None] == 1)
    slot = jnp.arange(NBR, dtype=jnp.int32)[None, None, :]
    order = jnp.argsort(jnp.where(valid, slot, NBR + slot), axis=-1, stable=True)
    picked = jnp.take_along_axis(jnp.broadcast_to(candidate[None], valid.shape), order, axis=-1)
    kept = jnp.take_along_axis(valid, order, axis=-1)
    lists = jnp.where(kept, picked, -1).astype(jnp.int32)
    return (alive, lists)


def draw_neighbours(key, part):
    alive, lists = structure(key)
    return lists


def draw_active(key, part):
    alive, lists = structure(key)
    return alive


def draw_w_qkv(key, part):
    key = jax.random.fold_in(key, 11)
    first = jax.random.fold_in(key, 0)
    base = jnp.clip(jax.random.normal(first, (D, 3 * D)), -6.0, 6.0) * D ** (-0.5)
    return base.astype(jnp.bfloat16)


def block_levels(own_key, shape, shards, least, high):
    loudness, own = 1.0, jax.random.fold_in(own_key, 6)
    for position, shards_of in shards:
        steps = jnp.exp(jax.random.uniform(jax.random.fold_in(own, position), (shards_of,), jnp.float32, least / len(shards), high / len(shards)))
        loudness = loudness * jnp.repeat(steps, shape[position] // shards_of).reshape([-1 if axis == position else 1 for axis in range(len(shape))])
    return loudness


def scatter_about(rng, dims, width, bound, shards=(), kind=jnp.bfloat16):
    loudness = block_levels(rng, dims, shards, -0.22, 0.18) if shards else 1.0
    entries = jax.random.normal(rng, dims, jnp.float32) * width * loudness
    return jnp.minimum(jnp.maximum(entries, -bound), bound).astype(kind)


def setup_inputs(seed: int = 0) -> dict:
    splits = jax.random.split(jax.random.key(seed), 8)
    return {
        "tokens": scatter_about(splits[0], (REGIONS, TOK_REGION, D), 1.0, 6.0, ((0, 8), (1, 64))),
        "cotangent": scatter_about(splits[1], (REGIONS, TOK_REGION, D), 1.0, 6.0, ((0, 8), (1, 64))),
        "neighbours": draw_neighbours(jax.random.fold_in(splits[7], 71), 0),
        "active": draw_active(jax.random.fold_in(splits[7], 71), 0),
        "gain": jnp.clip(1.0 + 0.18 * jax.random.normal(splits[4], (D,), jnp.float32), 0.1, 1.9),
        "w_qkv": draw_w_qkv(jax.random.fold_in(splits[7], 71), 0),
        "w_out": scatter_about(splits[6], (D, D), D ** -0.5, 0.3125),
    }


def normalize(values, gain):
    power = lax.optimization_barrier(jnp.mean(values * values, axis=1, keepdims=True))
    return values * lax.rsqrt(power + 1e-06) * gain

def block_mask(lists, table_ids):
    listed = lists[:, :, None]
    hit = (listed == table_ids[None, None, :]) & (listed >= 0)
    return jnp.any(hit, axis=1)

def inner(left, right):
    return lax.dot_general(left, right, (((1,), (1,)), ((), ())), preferred_element_type=jnp.float32)

def across(left, right):
    return lax.dot_general(left, right, (((0,), (0,)), ((), ())), preferred_element_type=jnp.float32)

def attend(queries, table, blockmask):
    rows, border_width = queries.shape
    head_size = border_width // HEADS
    nqb, ntb = blockmask.shape
    block = rows // nqb
    keys = table.shape[0]
    factor = 1.0 / head_size ** 0.5
    outputs = []
    weights = []
    for head in range(HEADS):
        lo = head * head_size
        scores = inner(queries[:, lo:lo + head_size], table[:, lo:lo + head_size]) * factor
        scores = jnp.where(blockmask[:, None, :, None], scores.reshape(nqb, block, ntb, block), -1e+30).reshape(rows, keys)
        top = lax.stop_gradient(lax.optimization_barrier(jnp.max(scores, axis=1, keepdims=True)))
        expo = jnp.exp(scores - top)
        share = (expo / lax.optimization_barrier(jnp.sum(expo, axis=1, keepdims=True))).astype(jnp.bfloat16)
        outputs.append(jnp.dot(share, table[:, border_width + lo:border_width + lo + head_size], preferred_element_type=jnp.float32))
        weights.append(share)
    return (jnp.concatenate(outputs, axis=1).astype(jnp.bfloat16), weights)

def attend_back(d_attn, queries, table, weights):
    rows, border_width = queries.shape
    head_size = border_width // HEADS
    factor = 1.0 / head_size ** 0.5
    dq_parts = []
    dk_parts = []
    dv_parts = []
    for head in range(HEADS):
        lo = head * head_size
        grad_out = d_attn[:, lo:lo + head_size]
        share = weights[head]
        d_share = inner(grad_out, table[:, border_width + lo:border_width + lo + head_size])
        share32 = share.astype(jnp.float32)
        d_scores = (share32 * (d_share - lax.optimization_barrier(jnp.sum(share32 * d_share, axis=1, keepdims=True))) * factor).astype(jnp.bfloat16)
        dq_parts.append(jnp.dot(d_scores, table[:, lo:lo + head_size], preferred_element_type=jnp.float32))
        dk_parts.append(across(d_scores, queries[:, lo:lo + head_size]))
        dv_parts.append(across(share, grad_out))
    d_queries = jnp.concatenate(dq_parts, axis=1).astype(jnp.bfloat16)
    d_table = jnp.concatenate(dk_parts + dv_parts, axis=1).astype(jnp.bfloat16)
    return (d_queries, d_table)

def build_neighbour_windows(slab_split_tokens, boundary_plane):
    border_width = slab_split_tokens.shape[2]
    empty_rim = jnp.zeros((1, boundary_plane, border_width), slab_split_tokens.dtype)
    lower_border = jnp.concatenate([empty_rim, slab_split_tokens[:-1, SLAB_TOKENS - boundary_plane:]], axis=0)
    upper_border = jnp.concatenate([slab_split_tokens[1:, :boundary_plane], empty_rim], axis=0)
    return jnp.concatenate([lower_border, slab_split_tokens, upper_border], axis=1)

def reference(tokens, cotangent, neighbours, active, gain, w_qkv, w_out):
    slabs = NBLK // BPD
    side = GY * GZ
    boundary_plane = side * BT
    w_keyval = w_qkv[:, D:]

    def region_pass(items):
        values, cot, lists, act = items
        values32 = values.astype(jnp.float32)
        normed = normalize(values32, gain).astype(jnp.bfloat16)
        queries = jnp.dot(normed, w_qkv[:, :D], preferred_element_type=jnp.float32).astype(jnp.bfloat16)
        keyval = jnp.dot(normed, w_keyval, preferred_element_type=jnp.float32).astype(jnp.bfloat16)
        windows = build_neighbour_windows(keyval.reshape(slabs, SLAB_TOKENS, 2 * D), boundary_plane)
        normed_windows = build_neighbour_windows(normed.reshape(slabs, SLAB_TOKENS, D), boundary_plane)
        scaled = (cot.reshape(NBLK, BT, D) * act.astype(jnp.bfloat16)[:, None, None]).reshape(TOK_REGION, D)
        d_attn = jnp.dot(scaled, w_out.T, preferred_element_type=jnp.float32).astype(jnp.bfloat16)
        ids = (jnp.arange(slabs)[:, None] * BPD - side + jnp.arange(BPD + 2 * side)[None, :]).astype(jnp.int32)
        masks = jax.vmap(block_mask)(lists.reshape(slabs, BPD, NBR), ids)

        def one_slab(piece):
            slab_q, slab_table, slab_normed, slab_mask, slab_grad = piece
            attn, weights = attend(slab_q, slab_table, slab_mask)
            d_queries, d_table = attend_back(slab_grad, slab_q, slab_table, weights)
            grad_kv = across(slab_normed, d_table)
            own = inner(d_table[boundary_plane:boundary_plane + SLAB_TOKENS], w_keyval)
            lower = inner(d_table[:boundary_plane], w_keyval).astype(jnp.bfloat16)
            upper = inner(d_table[boundary_plane + SLAB_TOKENS:], w_keyval).astype(jnp.bfloat16)
            return (attn, d_queries, grad_kv, own, lower, upper)
        attn, d_queries, grad_kv, own, lower, upper = lax.map(one_slab, (queries.reshape(slabs, SLAB_TOKENS, D), windows, normed_windows, masks, d_attn.reshape(slabs, SLAB_TOKENS, D)))
        blank32 = jnp.zeros((1, boundary_plane, D), jnp.float32)
        lower = lower.astype(jnp.float32)
        upper = upper.astype(jnp.float32)
        kv_back = own.at[:, SLAB_TOKENS - boundary_plane:].add(jnp.concatenate([lower[1:], blank32], axis=0))
        kv_back = kv_back.at[:, :boundary_plane].add(jnp.concatenate([blank32, upper[:-1]], axis=0))
        kv_back = kv_back.reshape(TOK_REGION, D)
        attn = attn.reshape(TOK_REGION, D)
        d_queries = d_queries.reshape(TOK_REGION, D)
        grad_wout = across(attn, scaled)
        grad_wqkv = jnp.concatenate([across(normed, d_queries), lax.optimization_barrier(jnp.sum(grad_kv, axis=0))], axis=1)
        d_normed = (inner(d_queries, w_qkv[:, :D]) + kv_back).astype(jnp.bfloat16)
        unused, pullback = jax.vjp(normalize, values32, gain)
        d_norm_in, d_gain = pullback(d_normed.astype(jnp.float32))
        grad_input = (cot.astype(jnp.float32) + d_norm_in).astype(jnp.bfloat16)
        return (grad_input, grad_wqkv, grad_wout, d_gain)
    grad_input, grad_wqkv, grad_wout, d_gain = lax.map(region_pass, (tokens, cotangent, neighbours, active))
    factor = 1.0 / (REGIONS * TOK_REGION) ** 0.5
    return (grad_input, lax.optimization_barrier(jnp.sum(grad_wqkv, axis=0)) * factor, lax.optimization_barrier(jnp.sum(grad_wout, axis=0)) * factor, lax.optimization_barrier(jnp.sum(d_gain, axis=0)) * factor)
```

```python
import math

import jax
import jax.numpy as jnp
from jax import lax
from jax.sharding import Mesh
from jax.sharding import PartitionSpec as P

HEADS = 6
SIDE = 9
SPACE = ("yh", "x", "z")


def inner(left, right):
    return lax.dot_general(
        left, right, (((1,), (1,)), ((), ())), preferred_element_type=jnp.float32
    )


def across(left, right):
    return lax.dot_general(
        left, right, (((0,), (0,)), ((), ())), preferred_element_type=jnp.float32
    )


def shifted(block, distance):
    count = lax.axis_size(SPACE)
    route = [(i, i + distance) for i in range(count) if 0 <= i + distance < count]
    return lax.ppermute(block, SPACE, route)


def spread(part, axes):
    count = lax.axis_size(axes)
    copies = jnp.broadcast_to(part[None], (count,) + part.shape)
    return lax.all_to_all(copies, axes, 0, 0, tiled=True)


def total(parts):
    return jnp.sum(parts.astype(jnp.float32), axis=0).astype(jnp.bfloat16)


def reduced(blocks):
    core = lax.axis_index("c")
    own = lax.dynamic_index_in_dim(blocks, core, 0, False)
    other = lax.dynamic_index_in_dim(blocks, 1 - core, 0, False)
    swap = [(0, 1), (1, 0)]
    half = total(jnp.stack([own, lax.ppermute(other, "c", swap)]))
    plane = lax.axis_size(("x", "z"))
    rows, columns = half.shape
    parts = half.reshape(plane, rows // plane, columns)
    part = total(lax.all_to_all(parts, ("x", "z"), 0, 0, tiled=True))
    part = total(spread(part, ("yl", "yh")))
    half = spread(part, ("x", "z")).reshape(rows, columns)
    other = lax.ppermute(half, "c", swap)
    return jnp.where(core == 0, jnp.stack([half, other]), jnp.stack([other, half]))


def shards(tokens, cotangent, neighbours, active, gain, w_qkv, w_out):
    values = tokens[0]
    cot = cotangent[0]
    lists = neighbours[0]
    alive = active[0]
    rows, width = values.shape
    nqb = alive.shape[0]
    block = rows // nqb
    head_size = width // HEADS
    factor = 1.0 / head_size**0.5
    position = lax.axis_index(SPACE)
    window = jnp.concatenate([shifted(values, 1), values, shifted(values, -1)], axis=0)
    window32 = window.astype(jnp.float32)
    root = lax.rsqrt(jnp.mean(window32 * window32, axis=1, keepdims=True) + 1e-06)
    normed = (window32 * root * gain).astype(jnp.bfloat16)
    own = normed[rows : 2 * rows]
    w_query = w_qkv[:, :width]
    w_keyval = w_qkv[:, width:]
    queries = jnp.dot(own, w_query, preferred_element_type=jnp.float32).astype(jnp.bfloat16)
    table = jnp.dot(normed, w_keyval, preferred_element_type=jnp.float32).astype(jnp.bfloat16)
    ids = position * nqb - SIDE + jnp.arange(nqb + 2 * SIDE)
    mask = jnp.any((lists[:, :, None] == ids[None, None, :]) & (lists[:, :, None] >= 0), axis=1)
    ntb = nqb + 2 * SIDE
    scaled = (
        cot.reshape(nqb, block, width) * alive.astype(jnp.bfloat16)[:, None, None]
    ).reshape(rows, width)
    d_attn = inner(scaled, w_out).astype(jnp.bfloat16)
    outs, dqs, dks, dvs = [], [], [], []
    for head in range(HEADS):
        at = slice(head * head_size, (head + 1) * head_size)
        q, k, v, g = queries[:, at], table[:, at], table[:, width:][:, at], d_attn[:, at]
        scores = inner(q, k) * factor
        scores = jnp.where(
            mask[:, None, :, None], scores.reshape(nqb, block, ntb, block), -1e30
        ).reshape(rows, -1)
        expo = jnp.exp(scores - jnp.max(scores, axis=1, keepdims=True))
        share = (expo / jnp.sum(expo, axis=1, keepdims=True)).astype(jnp.bfloat16)
        out = jnp.dot(share, v, preferred_element_type=jnp.float32)
        d_share = inner(g, v)
        share32 = share.astype(jnp.float32)
        delta = jnp.sum(share32 * d_share, axis=1, keepdims=True)
        d_scores = (share32 * (d_share - delta) * factor).astype(jnp.bfloat16)
        outs.append(out)
        dqs.append(jnp.dot(d_scores, k, preferred_element_type=jnp.float32))
        dks.append(across(d_scores, q))
        dvs.append(across(share, g))
    attn = jnp.concatenate(outs, axis=1).astype(jnp.bfloat16)
    d_queries = jnp.concatenate(dqs, axis=1).astype(jnp.bfloat16)
    d_table = jnp.concatenate(dks + dvs, axis=1).astype(jnp.bfloat16)
    back = inner(d_table, w_keyval)
    above = shifted(back[:rows].astype(jnp.bfloat16), -1)
    below = shifted(back[2 * rows :].astype(jnp.bfloat16), 1)
    grad_q = across(own, d_queries)
    grad_kv = across(normed, d_table)
    grad_out = across(attn, scaled)
    blocks = jnp.stack(
        [
            jnp.concatenate([grad_q, grad_kv[:, :width]], axis=0),
            jnp.concatenate([grad_kv[:, width:], grad_out], axis=0),
        ]
    ).astype(jnp.bfloat16)
    summed = reduced(blocks)
    d_normed = inner(d_queries, w_query) + back[rows : 2 * rows]
    d_normed = d_normed + above.astype(jnp.float32) + below.astype(jnp.float32)
    d_normed = d_normed.astype(jnp.bfloat16).astype(jnp.float32)
    own32 = window32[rows : 2 * rows]
    own_root = root[rows : 2 * rows]
    inward = d_normed * gain
    slope = jnp.mean(inward * own32, axis=1, keepdims=True) * own_root * own_root
    grad_input = cot.astype(jnp.float32) + own_root * (inward - own32 * slope)
    scale = 1.0 / math.sqrt(512 * rows)
    summed = summed.astype(jnp.float32) * scale
    grad_wqkv = jnp.concatenate([summed[0, :width], summed[0, width:], summed[1, :width]], axis=1)
    grad_gain = jnp.sum(grad_wqkv * w_qkv.astype(jnp.float32), axis=1) / gain
    return (grad_input.astype(jnp.bfloat16)[None], grad_wqkv, summed[1, width:], grad_gain)


def solution(mesh):
    fine = Mesh(mesh.devices.reshape(4, 2, 2, 4, 8), ("yl", "c", "yh", "x", "z"))
    region = ("yl", "c")
    split = P(region, SPACE, None)
    return jax.shard_map(
        shards,
        mesh=fine,
        in_specs=(split, split, split, P(region, SPACE), P(), P(), P()),
        out_specs=(split, P(), P(), P()),
        check_vma=False,
    )
```

```python
import math

import jax
import jax.numpy as jnp
from jax import lax
from jax.experimental import pallas as pl
from jax.experimental.pallas import tpu as pltpu
from jax.sharding import Mesh
from jax.sharding import PartitionSpec as P

HEADS = 6
SIDE = 9
ROWS = 288
WIDTH = 384
HEAD = 64
KEYS = 896
SPACE = ("yh", "x", "z")
HIDDEN = -1e30


def inner(left, right):
    return lax.dot_general(
        left, right, (((1,), (1,)), ((), ())), preferred_element_type=jnp.float32
    )


def dot(left, right):
    return jnp.dot(left, right, preferred_element_type=jnp.float32)


def swapped(block, first):
    count = lax.axis_size(SPACE)
    pairs = [(i, i + 1) for i in range(first, count - 1, 2)]
    return lax.ppermute(block, SPACE, pairs + [(b, a) for a, b in pairs])


def spread(part, axes):
    count = lax.axis_size(axes)
    copies = jnp.broadcast_to(part[None], (count,) + part.shape)
    return lax.all_to_all(copies, axes, 0, 0, tiled=True)


def total(parts):
    return jnp.sum(parts.astype(jnp.float32), axis=0).astype(jnp.bfloat16)


def attention_kernel(
    core, near, far, own, kv, q8, q8t, g, scaled, fq, fk, gain, wkv,
    out, dt, dq, normed, table, scores, expo, dshare, dscores,
):
    def unit(ref):
        values = ref[...].astype(jnp.float32)
        power = jnp.mean(values * values, axis=1, keepdims=True)
        return (values * lax.rsqrt(power + 1e-06) * gain[...]).astype(jnp.bfloat16)

    normed[0:ROWS] = own[...]
    normed[ROWS : 2 * ROWS] = unit(near)
    normed[2 * ROWS : 3 * ROWS] = unit(far)
    normed[3 * ROWS : KEYS] = jnp.zeros((KEYS - 3 * ROWS, WIDTH), jnp.bfloat16)
    table[0:ROWS] = kv[...]
    table[ROWS : 3 * ROWS] = dot(normed[ROWS : 3 * ROWS], wkv[...]).astype(jnp.bfloat16)
    table[3 * ROWS : KEYS] = jnp.zeros((KEYS - 3 * ROWS, 2 * WIDTH), jnp.bfloat16)
    low = lax.broadcasted_iota(jnp.int32, (ROWS, 128), 1) < HEAD
    chunks = [slice(at, at + 32) for at in range(0, ROWS, 32)]
    attn = []
    for pair in range(HEADS // 2):
        lanes = slice(pair * 128, pair * 128 + 128)
        keys = table[:, lanes]
        values = table[:, WIDTH + pair * 128 : WIDTH + pair * 128 + 128]
        wide_keys = jnp.concatenate([keys, fk[...]], axis=1)
        outs, grads, dqs = [], [], []
        for half in range(2):
            head = 2 * pair + half
            keep = low if half == 0 else jnp.logical_not(low)
            zero = jnp.zeros((ROWS, 128), jnp.float32)
            queries = jnp.where(keep, q8[:, lanes].astype(jnp.float32), zero)
            queries = jnp.concatenate([queries.astype(jnp.bfloat16), fq[...]], axis=1)
            scores[half] = inner(queries, wide_keys)
            shares = []
            for rows in chunks:
                block = scores[half, rows]
                block = jnp.exp(block - jnp.max(block, axis=1, keepdims=True))
                shares.append(1.0 / jnp.sum(block, axis=1, keepdims=True))
                expo[half, rows] = block.astype(jnp.bfloat16)
            share = jnp.concatenate(shares, axis=0)
            result = dot(expo[half], values) * share
            grad = jnp.where(keep, g[:, lanes] * share, zero).astype(jnp.bfloat16)
            delta = jnp.sum(grad.astype(jnp.float32) * result, axis=1, keepdims=True)
            dshare[half] = inner(grad, values)
            for rows in chunks:
                block = expo[half, rows].astype(jnp.float32)
                block = block * (dshare[half, rows] - delta[rows])
                dscores[half, rows] = block.astype(jnp.bfloat16)
            dqs.append(dot(dscores[half], keys) * (1.0 / math.sqrt(HEAD)))
            at = slice(head * HEAD, head * HEAD + HEAD)
            dt[at] = dot(q8t[at], dscores[half]).astype(jnp.bfloat16)
            outs.append(result)
            grads.append(grad)
        attn.append(jnp.where(low, outs[0], outs[1]).astype(jnp.bfloat16))
        dq[:, lanes] = jnp.where(low, dqs[0], dqs[1]).astype(jnp.bfloat16)
        turned = (grads[0] + grads[1]).T
        for half in range(2):
            at = WIDTH + (2 * pair + half) * HEAD
            part = turned[half * HEAD : half * HEAD + HEAD]
            dt[at : at + HEAD] = dot(part, expo[half]).astype(jnp.bfloat16)
    mine = core[0]
    normed_t = normed[...].T
    out[mine, 0:WIDTH] = dot(normed[0:ROWS].T, dq[...]).astype(jnp.bfloat16)
    out[mine, WIDTH:] = inner(normed_t, dt[0:WIDTH]).astype(jnp.bfloat16)
    out[1 - mine, 0:WIDTH] = inner(normed_t, dt[WIDTH:]).astype(jnp.bfloat16)
    attn_t = jnp.concatenate(attn, axis=1).T
    out[1 - mine, WIDTH:] = dot(attn_t, scaled[...]).astype(jnp.bfloat16)


def output_kernel(core, mine, other, wqkv, gain, grad_qkv, grad_out, grad_gain):
    scale = 1.0 / math.sqrt(512 * ROWS)
    me = core[0]

    def halves(first, second):
        query = first[0:WIDTH].astype(jnp.float32) * scale
        key = first[WIDTH:].astype(jnp.float32) * scale
        value = second[0:WIDTH].astype(jnp.float32) * scale
        grad_qkv[:, 0:WIDTH] = query
        grad_qkv[:, WIDTH : 2 * WIDTH] = key
        grad_qkv[:, 2 * WIDTH :] = value
        grad_out[...] = second[WIDTH:].astype(jnp.float32) * scale
        moved = query * wqkv[:, 0:WIDTH].astype(jnp.float32)
        moved += key * wqkv[:, WIDTH : 2 * WIDTH].astype(jnp.float32)
        moved += value * wqkv[:, 2 * WIDTH :].astype(jnp.float32)
        grad_gain[...] = jnp.sum(moved.T, axis=0, keepdims=True) / gain[...]

    @pl.when(me == 0)
    def _():
        halves(mine, other)

    @pl.when(me == 1)
    def _():
        halves(other, mine)


def shards(tokens, cotangent, neighbours, active, gain, w_qkv, w_out):
    values = tokens[0]
    cot = cotangent[0]
    lists = neighbours[0]
    alive = active[0]
    block = ROWS // SIDE
    position = lax.axis_index(SPACE)
    core = lax.axis_index("c")
    near = swapped(values, 0)
    far = swapped(values, 1)

    values32 = values.astype(jnp.float32)
    root = lax.rsqrt(jnp.mean(values32 * values32, axis=1, keepdims=True) + 1e-06)
    own = (values32 * root * gain).astype(jnp.bfloat16)
    w_query = w_qkv[:, :WIDTH]
    w_keyval = w_qkv[:, WIDTH:]
    q8 = (dot(own, w_query).astype(jnp.bfloat16) * (1.0 / math.sqrt(HEAD))).astype(jnp.bfloat16)
    kv = dot(own, w_keyval).astype(jnp.bfloat16)
    scaled = (
        cot.reshape(SIDE, block, WIDTH) * alive.astype(jnp.bfloat16)[:, None, None]
    ).reshape(ROWS, WIDTH)
    d_attn = inner(scaled, w_out).astype(jnp.bfloat16).astype(jnp.float32)
    parity = position % 2
    slabs = jnp.stack([position, position + 1 - 2 * parity, position - 1 + 2 * parity])
    ids = (slabs[:, None] * SIDE + jnp.arange(SIDE)[None, :]).reshape(-1)
    seen = jnp.any((lists[:, :, None] == ids) & (lists[:, :, None] >= 0), axis=1)
    hidden = jnp.where(seen, 0.0, HIDDEN).T.astype(jnp.bfloat16)
    fk = jnp.pad(jnp.repeat(hidden, block, axis=0), ((0, KEYS - 3 * ROWS), (0, 0)), constant_values=HIDDEN)
    fk = jnp.pad(fk, ((0, 0), (0, 128 - SIDE)))
    row_block = lax.broadcasted_iota(jnp.int32, (ROWS, 128), 0) // block
    fq = (row_block == lax.broadcasted_iota(jnp.int32, (ROWS, 128), 1)).astype(jnp.bfloat16)

    whole = pl.BlockSpec(memory_space=pltpu.VMEM)
    scalar = pl.BlockSpec(memory_space=pltpu.SMEM)
    core_ref = jnp.reshape(core, (1,)).astype(jnp.int32)
    blocks, d_table, d_queries = pl.pallas_call(
        attention_kernel,
        out_shape=(
            jax.ShapeDtypeStruct((2, 2 * WIDTH, WIDTH), jnp.bfloat16),
            jax.ShapeDtypeStruct((2 * WIDTH, KEYS), jnp.bfloat16),
            jax.ShapeDtypeStruct((ROWS, WIDTH), jnp.bfloat16),
        ),
        in_specs=[scalar] + [whole] * 12,
        out_specs=(whole,) * 3,
        scratch_shapes=[
            pltpu.VMEM((KEYS, WIDTH), jnp.bfloat16),
            pltpu.VMEM((KEYS, 2 * WIDTH), jnp.bfloat16),
            pltpu.VMEM((2, ROWS, KEYS), jnp.float32),
            pltpu.VMEM((2, ROWS, KEYS), jnp.bfloat16),
            pltpu.VMEM((2, ROWS, KEYS), jnp.float32),
            pltpu.VMEM((2, ROWS, KEYS), jnp.bfloat16),
        ],
        compiler_params=pltpu.CompilerParams(vmem_limit_bytes=40 * 2**20),
        cost_estimate=pl.CostEstimate(flops=3 * 10**9, bytes_accessed=4 * 10**6, transcendentals=1500000),
        name="attention",
    )(core_ref, near, far, own, kv, q8, q8.T, d_attn, scaled, fq, fk, gain[None], w_keyval)

    pair = [(0, 1), (1, 0)]
    half = total(jnp.stack([blocks[0], lax.ppermute(blocks[1], "c", pair)]))
    plane = lax.axis_size(("x", "z"))
    parts = half.reshape(plane, 2 * WIDTH // plane, WIDTH)
    part = total(lax.all_to_all(parts, ("x", "z"), 0, 0, tiled=True))
    part = total(spread(part, ("yl", "yh")))
    half = spread(part, ("x", "z")).reshape(2 * WIDTH, WIDTH)
    other = lax.ppermute(half, "c", pair)

    back = lax.dot_general(
        d_table, w_keyval, (((0,), (1,)), ((), ())), preferred_element_type=jnp.float32
    )
    back_near = swapped(back[ROWS : 2 * ROWS].astype(jnp.bfloat16), 0)
    back_far = swapped(back[2 * ROWS : 3 * ROWS].astype(jnp.bfloat16), 1)
    d_normed = inner(d_queries, w_query) + back[:ROWS]
    d_normed = d_normed + back_near.astype(jnp.float32) + back_far.astype(jnp.float32)
    d_normed = d_normed.astype(jnp.bfloat16).astype(jnp.float32)
    inward = d_normed * gain
    slope = jnp.mean(inward * values32, axis=1, keepdims=True) * root * root
    grad_input = cot.astype(jnp.float32) + root * (inward - values32 * slope)

    grad_wqkv, grad_wout, grad_gain = pl.pallas_call(
        output_kernel,
        out_shape=(
            jax.ShapeDtypeStruct((WIDTH, 3 * WIDTH), jnp.float32),
            jax.ShapeDtypeStruct((WIDTH, WIDTH), jnp.float32),
            jax.ShapeDtypeStruct((1, WIDTH), jnp.float32),
        ),
        in_specs=[scalar] + [whole] * 4,
        out_specs=(whole,) * 3,
        compiler_params=pltpu.CompilerParams(vmem_limit_bytes=24 * 2**20),
        name="outputs",
    )(core_ref, half, other, w_qkv, gain[None])
    return (grad_input.astype(jnp.bfloat16)[None], grad_wqkv, grad_wout, grad_gain[0])


def solution(mesh):
    fine = Mesh(mesh.devices.reshape(4, 2, 2, 4, 8), ("yl", "c", "yh", "x", "z"))
    region = ("yl", "c")
    split = P(region, SPACE, None)
    return jax.shard_map(
        shards,
        mesh=fine,
        in_specs=(split, split, split, P(region, SPACE), P(), P(), P()),
        out_specs=(split, P(), P(), P()),
        check_vma=False,
    )
```

```python
import math

import jax
import jax.numpy as jnp
from jax import lax
from jax.experimental import pallas as pl
from jax.experimental.pallas import tpu as pltpu
from jax.sharding import Mesh
from jax.sharding import PartitionSpec as P

HEADS = 6
SIDE = 9
ROWS = 288
WIDTH = 384
HEAD = 64
KEYS = 896
SPACE = ("yh", "x", "z")
HIDDEN = -1e30


def inner(left, right):
    return lax.dot_general(
        left, right, (((1,), (1,)), ((), ())), preferred_element_type=jnp.float32
    )


def dot(left, right):
    return jnp.dot(left, right, preferred_element_type=jnp.float32)


def swapped(block, first):
    count = lax.axis_size(SPACE)
    pairs = [(i, i + 1) for i in range(first, count - 1, 2)]
    return lax.ppermute(block, SPACE, pairs + [(b, a) for a, b in pairs])


def spread(part, axes):
    count = lax.axis_size(axes)
    copies = jnp.broadcast_to(part[None], (count,) + part.shape)
    return lax.all_to_all(copies, axes, 0, 0, tiled=True)


def total(parts):
    return jnp.sum(parts.astype(jnp.float32), axis=0).astype(jnp.bfloat16)


def unit_rows(values, gain):
    power = jnp.mean(values * values, axis=1, keepdims=True)
    return values * lax.rsqrt(power + 1e-06) * gain


def prepare_kernel(alive, tokens, cot, gain, wqkv, wout, own, kv, q8, q8t, g, scaled):
    own[...] = unit_rows(tokens[...].astype(jnp.float32), gain[...]).astype(jnp.bfloat16)
    queries = dot(own[...], wqkv[:, 0:WIDTH]).astype(jnp.bfloat16).astype(jnp.float32)
    eighth = (queries * (1.0 / math.sqrt(HEAD))).astype(jnp.bfloat16)
    q8[...] = eighth
    q8t[...] = eighth.T
    kv[...] = dot(own[...], wqkv[:, WIDTH:]).astype(jnp.bfloat16)
    block = ROWS // SIDE
    for at in range(SIDE):
        rows = slice(at * block, at * block + block)
        part = cot[rows].astype(jnp.float32) * alive[at].astype(jnp.float32)
        scaled[rows] = part.astype(jnp.bfloat16)
    g[...] = inner(scaled[...], wout[...]).astype(jnp.bfloat16)


def attention_kernel(
    core, near, far, own, kv, q8, q8t, g, scaled, fq, fk, gain, wqkv,
    out, dt, dq, halo, normed, table, scores, expo, dshare, dscores, sems,
):
    copies = [
        pltpu.make_async_copy(near, halo.at[0], sems.at[0]),
        pltpu.make_async_copy(far, halo.at[1], sems.at[1]),
    ]
    for copy in copies:
        copy.start()
    normed[0:ROWS] = own[...]
    normed[3 * ROWS : KEYS] = jnp.zeros((KEYS - 3 * ROWS, WIDTH), jnp.bfloat16)
    table[0:ROWS] = kv[...]
    table[3 * ROWS : KEYS] = jnp.zeros((KEYS - 3 * ROWS, 2 * WIDTH), jnp.bfloat16)
    for side in range(2):
        copies[side].wait()
        rows = slice((side + 1) * ROWS, (side + 2) * ROWS)
        unit = unit_rows(halo[side].astype(jnp.float32), gain[...]).astype(jnp.bfloat16)
        normed[rows] = unit
        table[rows] = dot(unit, wqkv[:, WIDTH:]).astype(jnp.bfloat16)
    low = lax.broadcasted_iota(jnp.int32, (ROWS, 128), 1) < HEAD
    zero = jnp.zeros((ROWS, 128), jnp.float32)
    chunks = [slice(at, at + 32) for at in range(0, ROWS, 32)]
    attn = []
    for pair in range(HEADS // 2):
        lanes = slice(pair * 128, pair * 128 + 128)
        keys = table[:, lanes]
        values = table[:, WIDTH + pair * 128 : WIDTH + pair * 128 + 128]
        wide_keys = jnp.concatenate([keys, fk[...]], axis=1)
        outs, grads, dqs = [], [], []
        for half in range(2):
            head = 2 * pair + half
            keep = low if half == 0 else jnp.logical_not(low)
            queries = jnp.where(keep, q8[:, lanes].astype(jnp.float32), zero)
            queries = jnp.concatenate([queries.astype(jnp.bfloat16), fq[...]], axis=1)
            scores[half] = inner(queries, wide_keys)
            shares = []
            for rows in chunks:
                block = scores[half, rows]
                block = jnp.exp(block - jnp.max(block, axis=1, keepdims=True))
                shares.append(1.0 / jnp.sum(block, axis=1, keepdims=True))
                expo[half, rows] = block.astype(jnp.bfloat16)
            share = jnp.concatenate(shares, axis=0)
            result = dot(expo[half], values) * share
            grad = jnp.where(keep, g[:, lanes].astype(jnp.float32) * share, zero)
            grad = grad.astype(jnp.bfloat16)
            delta = jnp.sum(grad.astype(jnp.float32) * result, axis=1, keepdims=True)
            dshare[half] = inner(grad, values)
            for rows in chunks:
                block = expo[half, rows].astype(jnp.float32)
                block = block * (dshare[half, rows] - delta[rows])
                dscores[half, rows] = block.astype(jnp.bfloat16)
            dqs.append(dot(dscores[half], keys) * (1.0 / math.sqrt(HEAD)))
            at = slice(head * HEAD, head * HEAD + HEAD)
            dt[at] = dot(q8t[at], dscores[half]).astype(jnp.bfloat16)
            outs.append(result)
            grads.append(grad)
        attn.append(jnp.where(low, outs[0], outs[1]).astype(jnp.bfloat16))
        dq[:, lanes] = jnp.where(low, dqs[0], dqs[1]).astype(jnp.bfloat16)
        turned = (grads[0] + grads[1]).T
        for half in range(2):
            at = WIDTH + (2 * pair + half) * HEAD
            part = turned[half * HEAD : half * HEAD + HEAD]
            dt[at : at + HEAD] = dot(part, expo[half]).astype(jnp.bfloat16)
    mine = core[0]
    normed_t = normed[...].T
    out[mine, 0:WIDTH] = dot(normed[0:ROWS].T, dq[...]).astype(jnp.bfloat16)
    out[mine, WIDTH:] = inner(normed_t, dt[0:WIDTH]).astype(jnp.bfloat16)
    out[1 - mine, 0:WIDTH] = inner(normed_t, dt[WIDTH:]).astype(jnp.bfloat16)
    attn_t = jnp.concatenate(attn, axis=1).T
    out[1 - mine, WIDTH:] = dot(attn_t, scaled[...]).astype(jnp.bfloat16)


def back_kernel(dt, dq, wqkv, base, near, far):
    back = lax.dot_general(
        dt[...], wqkv[:, WIDTH:], (((0,), (1,)), ((), ())), preferred_element_type=jnp.float32
    )
    near[...] = back[ROWS : 2 * ROWS].astype(jnp.bfloat16)
    far[...] = back[2 * ROWS : 3 * ROWS].astype(jnp.bfloat16)
    base[...] = back[0:ROWS] + inner(dq[...], wqkv[:, 0:WIDTH])


def input_kernel(base, near, far, tokens, cot, gain, grad_input):
    d_normed = base[...] + near[...].astype(jnp.float32) + far[...].astype(jnp.float32)
    inward = d_normed.astype(jnp.bfloat16).astype(jnp.float32) * gain[...]
    values = tokens[...].astype(jnp.float32)
    root = lax.rsqrt(jnp.mean(values * values, axis=1, keepdims=True) + 1e-06)
    slope = jnp.mean(inward * values, axis=1, keepdims=True) * root * root
    moved = cot[...].astype(jnp.float32) + root * (inward - values * slope)
    grad_input[...] = moved.astype(jnp.bfloat16)


def output_kernel(core, mine, other, wqkv, gain, grad_qkv, grad_out, grad_gain):
    scale = 1.0 / math.sqrt(512 * ROWS)
    me = core[0]

    def halves(first, second):
        query = first[0:WIDTH].astype(jnp.float32) * scale
        key = first[WIDTH:].astype(jnp.float32) * scale
        value = second[0:WIDTH].astype(jnp.float32) * scale
        grad_qkv[:, 0:WIDTH] = query
        grad_qkv[:, WIDTH : 2 * WIDTH] = key
        grad_qkv[:, 2 * WIDTH :] = value
        grad_out[...] = second[WIDTH:].astype(jnp.float32) * scale
        moved = query * wqkv[:, 0:WIDTH].astype(jnp.float32)
        moved += key * wqkv[:, WIDTH : 2 * WIDTH].astype(jnp.float32)
        moved += value * wqkv[:, 2 * WIDTH :].astype(jnp.float32)
        grad_gain[...] = jnp.sum(moved.T, axis=0) / gain[...]

    @pl.when(me == 0)
    def _():
        halves(mine, other)

    @pl.when(me == 1)
    def _():
        halves(other, mine)


def local(body, name, shapes, in_specs, vmem, scratch=(), flops=10**8, moved=10**6):
    return pl.pallas_call(
        body,
        out_shape=tuple(jax.ShapeDtypeStruct(shape, kind) for shape, kind in shapes),
        in_specs=in_specs,
        out_specs=(pl.BlockSpec(memory_space=pltpu.VMEM),) * len(shapes),
        scratch_shapes=scratch,
        compiler_params=pltpu.CompilerParams(vmem_limit_bytes=vmem * 2**20),
        cost_estimate=pl.CostEstimate(flops=flops, bytes_accessed=moved, transcendentals=0),
        name=name,
    )


def shards(tokens, cotangent, neighbours, active, gain, w_qkv, w_out):
    values = tokens[0]
    cot = cotangent[0]
    lists = neighbours[0]
    block = ROWS // SIDE
    position = lax.axis_index(SPACE)
    core = jnp.reshape(lax.axis_index("c"), (1,)).astype(jnp.int32)
    near = swapped(values, 0)
    far = swapped(values, 1)
    gains = gain[None]

    b16, f32 = jnp.bfloat16, jnp.float32
    whole = pl.BlockSpec(memory_space=pltpu.VMEM)
    scalar = pl.BlockSpec(memory_space=pltpu.SMEM)
    anywhere = pl.BlockSpec(memory_space=pl.ANY)
    rows = ((ROWS, WIDTH), b16)
    own, kv, q8, q8t, g, scaled = local(
        prepare_kernel,
        "prepare",
        (rows, ((ROWS, 2 * WIDTH), b16), rows, ((WIDTH, ROWS), b16), rows, rows),
        [scalar] + [whole] * 5,
        8,
        flops=4 * 10**8,
    )(active[0], values, cot, gains, w_qkv, w_out)

    parity = position % 2
    slabs = jnp.stack([position, position + 1 - 2 * parity, position - 1 + 2 * parity])
    ids = (slabs[:, None] * SIDE + jnp.arange(SIDE)[None, :]).reshape(-1)
    seen = jnp.any((lists[:, :, None] == ids) & (lists[:, :, None] >= 0), axis=1)
    hidden = jnp.where(seen, 0.0, HIDDEN).T.astype(b16)
    fk = jnp.repeat(hidden, block, axis=0)
    fk = jnp.pad(fk, ((0, KEYS - 3 * ROWS), (0, 0)), constant_values=HIDDEN)
    fk = jnp.pad(fk, ((0, 0), (0, 128 - SIDE)))
    row_block = lax.broadcasted_iota(jnp.int32, (ROWS, 128), 0) // block
    fq = (row_block == lax.broadcasted_iota(jnp.int32, (ROWS, 128), 1)).astype(b16)

    blocks, d_table, d_queries = local(
        attention_kernel,
        "attention",
        (((2, 2 * WIDTH, WIDTH), b16), ((2 * WIDTH, KEYS), b16), rows),
        [scalar, anywhere, anywhere] + [whole] * 10,
        14,
        (
            pltpu.VMEM((2, ROWS, WIDTH), b16),
            pltpu.VMEM((KEYS, WIDTH), b16),
            pltpu.VMEM((KEYS, 2 * WIDTH), b16),
            pltpu.VMEM((2, ROWS, KEYS), f32),
            pltpu.VMEM((2, ROWS, KEYS), b16),
            pltpu.VMEM((2, ROWS, KEYS), f32),
            pltpu.VMEM((2, ROWS, KEYS), b16),
            pltpu.SemaphoreType.DMA((2,)),
        ),
        flops=3 * 10**9,
        moved=4 * 10**6,
    )(core, near, far, own, kv, q8, q8t, g, scaled, fq, fk, gains, w_qkv)

    pair = [(0, 1), (1, 0)]
    half = total(jnp.stack([blocks[0], lax.ppermute(blocks[1], "c", pair)]))
    base, back_near, back_far = local(
        back_kernel, "back", (((ROWS, WIDTH), f32), rows, rows), [whole] * 3, 8, flops=6 * 10**8
    )(d_table, d_queries, w_qkv)
    half, base, back_near, back_far = lax.optimization_barrier((half, base, back_near, back_far))
    back_near = swapped(back_near, 0)
    back_far = swapped(back_far, 1)
    plane = lax.axis_size(("x", "z"))
    parts = half.reshape(plane, 2 * WIDTH // plane, WIDTH)
    part = total(lax.all_to_all(parts, ("x", "z"), 0, 0, tiled=True))
    part, back_near, back_far = lax.optimization_barrier((part, back_near, back_far))
    (grad_input,) = local(input_kernel, "grad_input", (rows,), [whole] * 6, 8, moved=3 * 10**7)(
        base, back_near, back_far, values, cot, gains
    )
    part = total(spread(part, ("yl", "yh")))
    half = spread(part, ("x", "z")).reshape(2 * WIDTH, WIDTH)
    half, grad_input = lax.optimization_barrier((half, grad_input))
    other = lax.ppermute(half, "c", pair)

    grad_wqkv, grad_wout, grad_gain = local(
        output_kernel,
        "outputs",
        (((WIDTH, 3 * WIDTH), f32), ((WIDTH, WIDTH), f32), ((WIDTH,), f32)),
        [scalar] + [whole] * 4,
        8,
        moved=4 * 10**6,
    )(core, half, other, w_qkv, gain)
    return (grad_input[None], grad_wqkv, grad_wout, grad_gain)


def solution(mesh):
    fine = Mesh(mesh.devices.reshape(4, 2, 2, 4, 8), ("yl", "c", "yh", "x", "z"))
    region = ("yl", "c")
    split = P(region, SPACE, None)
    return jax.shard_map(
        shards,
        mesh=fine,
        in_specs=(split, split, split, P(region, SPACE), P(), P(), P()),
        out_specs=(split, P(), P(), P()),
        check_vma=False,
    )
```

```python
import math

import jax
import jax.numpy as jnp
from jax import lax
from jax.experimental import pallas as pl
from jax.experimental.pallas import tpu as pltpu
from jax.sharding import Mesh
from jax.sharding import PartitionSpec as P

HEADS = 6
SIDE = 9
ROWS = 288
WIDTH = 384
HEAD = 64
KEYS = 896
SPACE = ("yh", "x", "z")
HIDDEN = -1e30


def inner(left, right):
    return lax.dot_general(
        left, right, (((1,), (1,)), ((), ())), preferred_element_type=jnp.float32
    )


def dot(left, right):
    return jnp.dot(left, right, preferred_element_type=jnp.float32)


def swapped(block, first):
    count = lax.axis_size(SPACE)
    pairs = [(i, i + 1) for i in range(first, count - 1, 2)]
    return lax.ppermute(block, SPACE, pairs + [(b, a) for a, b in pairs])


def spread(part, axes):
    count = lax.axis_size(axes)
    copies = jnp.broadcast_to(part[None], (count,) + part.shape)
    return lax.all_to_all(copies, axes, 0, 0, tiled=True)


def total(parts):
    return jnp.sum(parts.astype(jnp.float32), axis=0).astype(jnp.bfloat16)


def unit_rows(values, gain):
    power = jnp.mean(values * values, axis=1, keepdims=True)
    return values * lax.rsqrt(power + 1e-06) * gain


def fetch(pairs, sems):
    copies = [
        pltpu.make_async_copy(source, target, sems.at[i]) for i, (source, target) in enumerate(pairs)
    ]
    for copy in copies:
        copy.start()
    return copies


def prepare_kernel(
    alive, tokens_in, cot_in, gain, wqkv_in, wout_in, own, kv, q8, q8t, g, scaled,
    tokens, cot, wqkv, wout, sems,
):
    copies = fetch([(tokens_in, tokens), (wqkv_in, wqkv), (cot_in, cot), (wout_in, wout)], sems)
    copies[0].wait()
    own[...] = unit_rows(tokens[...].astype(jnp.float32), gain[...]).astype(jnp.bfloat16)
    copies[1].wait()
    queries = dot(own[...], wqkv[:, 0:WIDTH]).astype(jnp.bfloat16).astype(jnp.float32)
    eighth = (queries * (1.0 / math.sqrt(HEAD))).astype(jnp.bfloat16)
    q8[...] = eighth
    q8t[...] = eighth.T
    kv[...] = dot(own[...], wqkv[:, WIDTH:]).astype(jnp.bfloat16)
    copies[2].wait()
    block = ROWS // SIDE
    for at in range(SIDE):
        rows = slice(at * block, at * block + block)
        part = cot[rows].astype(jnp.float32) * alive[at].astype(jnp.float32)
        scaled[rows] = part.astype(jnp.bfloat16)
    copies[3].wait()
    g[...] = inner(scaled[...], wout[...]).astype(jnp.bfloat16)


def attention_kernel(
    core, near, far, own, kv, q8, q8t, g, scaled, fq, fk, gain, wqkv,
    send, dt, dq, normed_t, attn_t, normed, table, scores, expo, dshare, dscores,
):
    normed[0:ROWS] = own[...]
    normed[3 * ROWS : KEYS] = jnp.zeros((KEYS - 3 * ROWS, WIDTH), jnp.bfloat16)
    table[0:ROWS] = kv[...]
    table[3 * ROWS : KEYS] = jnp.zeros((KEYS - 3 * ROWS, 2 * WIDTH), jnp.bfloat16)
    for side, halo in enumerate((near, far)):
        rows = slice((side + 1) * ROWS, (side + 2) * ROWS)
        unit = unit_rows(halo[...].astype(jnp.float32), gain[...]).astype(jnp.bfloat16)
        normed[rows] = unit
        table[rows] = dot(unit, wqkv[:, WIDTH:]).astype(jnp.bfloat16)
    normed_t[...] = normed[...].T
    both = lax.broadcasted_iota(jnp.int32, (2 * ROWS, 128), 0) < ROWS
    low = lax.broadcasted_iota(jnp.int32, (2 * ROWS, 128), 1) < HEAD
    keep = both == low
    zero = jnp.zeros((2 * ROWS, 128), jnp.float32)
    chunks = [slice(at, at + 32) for at in range(0, 2 * ROWS, 32)]
    pairs = range(HEADS // 2)
    lanes = [slice(pair * 128, pair * 128 + 128) for pair in pairs]
    values = [slice(WIDTH + at.start, WIDTH + at.stop) for at in lanes]
    shares, results, grads, deltas = [], [], [], []

    def twice(block):
        return jnp.concatenate([block, block], axis=0).astype(jnp.float32)

    def joined(block):
        return jnp.where(low[:ROWS], block[:ROWS], block[ROWS:]).astype(jnp.bfloat16)

    for pair in pairs:
        queries = jnp.where(keep, twice(q8[:, lanes[pair]]), zero).astype(jnp.bfloat16)
        queries = jnp.concatenate([queries, jnp.concatenate([fq[...], fq[...]], axis=0)], axis=1)
        scores[pair] = inner(queries, jnp.concatenate([table[:, lanes[pair]], fk[...]], axis=1))
    for pair in pairs:
        share = []
        for rows in chunks:
            block = scores[pair, rows]
            block = jnp.exp(block - jnp.max(block, axis=1, keepdims=True))
            share.append(1.0 / jnp.sum(block, axis=1, keepdims=True))
            expo[pair, rows] = block.astype(jnp.bfloat16)
        shares.append(jnp.concatenate(share, axis=0))
    for pair in pairs:
        results.append(dot(expo[pair], table[:, values[pair]]) * shares[pair])
        grad = jnp.where(keep, twice(g[:, lanes[pair]]) * shares[pair], zero)
        grads.append(grad.astype(jnp.bfloat16))
        dshare[pair] = inner(grads[pair], table[:, values[pair]])
        delta = grads[pair].astype(jnp.float32) * results[pair]
        deltas.append(jnp.sum(delta, axis=1, keepdims=True))
    for pair in pairs:
        for rows in chunks:
                block = (dshare[pair, rows] - deltas[pair][rows]).astype(jnp.bfloat16)
                dscores[pair, rows] = expo[pair, rows] * block
    for pair in pairs:
        moved = dot(dscores[pair], table[:, lanes[pair]]) * (1.0 / math.sqrt(HEAD))
        dq[:, lanes[pair]] = joined(moved)
        attn_t[lanes[pair]] = joined(results[pair]).T
        turned = (grads[pair][:ROWS] + grads[pair][ROWS:]).T
        for half in range(2):
            rows = slice(half * ROWS, half * ROWS + ROWS)
            at = (2 * pair + half) * HEAD
            part = q8t[at : at + HEAD]
            dt[at : at + HEAD] = dot(part, dscores[pair, rows]).astype(jnp.bfloat16)
            part = turned[half * HEAD : half * HEAD + HEAD]
            at += WIDTH
            dt[at : at + HEAD] = dot(part, expo[pair, rows]).astype(jnp.bfloat16)

    @pl.when(core[0] == 0)
    def _():
        value_half(send, normed_t, dt, attn_t, scaled)

    @pl.when(core[0] == 1)
    def _():
        key_half(send, normed_t, dt, dq)


def key_half(out, normed_t, dt, dq):
    out[0:WIDTH] = dot(normed_t[:, 0:ROWS], dq[...]).astype(jnp.bfloat16)
    out[WIDTH:] = inner(normed_t[...], dt[0:WIDTH]).astype(jnp.bfloat16)


def value_half(out, normed_t, dt, attn_t, scaled):
    out[0:WIDTH] = inner(normed_t[...], dt[WIDTH:]).astype(jnp.bfloat16)
    out[WIDTH:] = dot(attn_t[...], scaled[...]).astype(jnp.bfloat16)


def back_kernel(core, dt, dq, normed_t, attn_t, scaled, wqkv, held, base, near, far):
    back = lax.dot_general(
        dt[...], wqkv[:, WIDTH:], (((0,), (1,)), ((), ())), preferred_element_type=jnp.float32
    )
    near[...] = back[ROWS : 2 * ROWS].astype(jnp.bfloat16)
    far[...] = back[2 * ROWS : 3 * ROWS].astype(jnp.bfloat16)
    base[...] = back[0:ROWS] + inner(dq[...], wqkv[:, 0:WIDTH])

    @pl.when(core[0] == 0)
    def _():
        key_half(held, normed_t, dt, dq)

    @pl.when(core[0] == 1)
    def _():
        value_half(held, normed_t, dt, attn_t, scaled)


def gather_kernel(parts, copies):
    part = jnp.sum(parts[...].astype(jnp.float32), axis=0).astype(jnp.bfloat16)
    copies[...] = jnp.broadcast_to(part[None], copies.shape)


def input_kernel(base, near, far, tokens, cot, gain, grad_input):
    d_normed = base[...] + near[...].astype(jnp.float32) + far[...].astype(jnp.float32)
    inward = d_normed.astype(jnp.bfloat16).astype(jnp.float32) * gain[...]
    values = tokens[...].astype(jnp.float32)
    root = lax.rsqrt(jnp.mean(values * values, axis=1, keepdims=True) + 1e-06)
    slope = jnp.mean(inward * values, axis=1, keepdims=True) * root * root
    moved = cot[...].astype(jnp.float32) + root * (inward - values * slope)
    grad_input[...] = moved.astype(jnp.bfloat16)


def output_kernel(core, mine, other, wqkv, gain, grad_qkv, grad_out, grad_gain):
    scale = 1.0 / math.sqrt(512 * ROWS)
    me = core[0]

    def halves(first, second):
        query = first[0:WIDTH].astype(jnp.float32) * scale
        key = first[WIDTH:].astype(jnp.float32) * scale
        value = second[0:WIDTH].astype(jnp.float32) * scale
        grad_qkv[:, 0:WIDTH] = query
        grad_qkv[:, WIDTH : 2 * WIDTH] = key
        grad_qkv[:, 2 * WIDTH :] = value
        grad_out[...] = second[WIDTH:].astype(jnp.float32) * scale
        moved = query * wqkv[:, 0:WIDTH].astype(jnp.float32)
        moved += key * wqkv[:, WIDTH : 2 * WIDTH].astype(jnp.float32)
        moved += value * wqkv[:, 2 * WIDTH :].astype(jnp.float32)
        grad_gain[...] = jnp.sum(moved.T, axis=0) / gain[...]

    @pl.when(me == 0)
    def _():
        halves(mine, other)

    @pl.when(me == 1)
    def _():
        halves(other, mine)


def local(body, name, shapes, in_specs, vmem, scratch=(), flops=10**8, moved=10**6):
    return pl.pallas_call(
        body,
        out_shape=tuple(jax.ShapeDtypeStruct(shape, kind) for shape, kind in shapes),
        in_specs=in_specs,
        out_specs=(pl.BlockSpec(memory_space=pltpu.VMEM),) * len(shapes),
        scratch_shapes=scratch,
        compiler_params=pltpu.CompilerParams(vmem_limit_bytes=vmem * 2**20),
        cost_estimate=pl.CostEstimate(flops=flops, bytes_accessed=moved, transcendentals=0),
        name=name,
    )


def shards(tokens, cotangent, neighbours, active, gain, w_qkv, w_out):
    values = tokens[0]
    cot = cotangent[0]
    lists = neighbours[0]
    block = ROWS // SIDE
    position = lax.axis_index(SPACE)
    core = jnp.reshape(lax.axis_index("c"), (1,)).astype(jnp.int32)
    near = swapped(values, 0)
    far = swapped(values, 1)
    gains = gain[None]

    b16, f32 = jnp.bfloat16, jnp.float32
    whole = pl.BlockSpec(memory_space=pltpu.VMEM)
    scalar = pl.BlockSpec(memory_space=pltpu.SMEM)
    outside = pl.BlockSpec(memory_space=pltpu.HBM)
    rows = ((ROWS, WIDTH), b16)
    half_rows = ((2 * WIDTH, WIDTH), b16)
    dma = pltpu.SemaphoreType.DMA
    own, kv, q8, q8t, g, scaled = local(
        prepare_kernel,
        "prepare",
        (rows, ((ROWS, 2 * WIDTH), b16), rows, ((WIDTH, ROWS), b16), rows, rows),
        [scalar, outside, outside, whole, outside, outside],
        8,
        (
            pltpu.VMEM((ROWS, WIDTH), b16),
            pltpu.VMEM((ROWS, WIDTH), b16),
            pltpu.VMEM((WIDTH, 3 * WIDTH), b16),
            pltpu.VMEM((WIDTH, WIDTH), b16),
            dma((4,)),
        ),
        flops=4 * 10**8,
    )(active[0], values, cot, gains, w_qkv, w_out)

    parity = position % 2
    slabs = jnp.stack([position, position + 1 - 2 * parity, position - 1 + 2 * parity])
    ids = (slabs[:, None] * SIDE + jnp.arange(SIDE)[None, :]).reshape(-1)
    seen = jnp.any((lists[:, :, None] == ids) & (lists[:, :, None] >= 0), axis=1)
    hidden = jnp.where(seen, 0.0, HIDDEN).T.astype(b16)
    fk = jnp.repeat(hidden, block, axis=0)
    fk = jnp.pad(fk, ((0, KEYS - 3 * ROWS), (0, 0)), constant_values=HIDDEN)
    fk = jnp.pad(fk, ((0, 0), (0, 128 - SIDE)))
    row_block = lax.broadcasted_iota(jnp.int32, (ROWS, 128), 0) // block
    fq = (row_block == lax.broadcasted_iota(jnp.int32, (ROWS, 128), 1)).astype(b16)

    pair_rows = (HEADS // 2, 2 * ROWS, KEYS)
    send, d_table, d_queries, normed_t, attn_t = local(
        attention_kernel,
        "attention",
        (half_rows, ((2 * WIDTH, KEYS), b16), rows, ((WIDTH, KEYS), b16), ((WIDTH, ROWS), b16)),
        [scalar] + [whole] * 12,
        32,
        (
            pltpu.VMEM((KEYS, WIDTH), b16),
            pltpu.VMEM((KEYS, 2 * WIDTH), b16),
            pltpu.VMEM(pair_rows, f32),
            pltpu.VMEM(pair_rows, b16),
            pltpu.VMEM(pair_rows, f32),
            pltpu.VMEM(pair_rows, b16),
        ),
        flops=3 * 10**9,
        moved=4 * 10**6,
    )(core, near, far, own, kv, q8, q8t, g, scaled, fq, fk, gains, w_qkv)

    pair = [(0, 1), (1, 0)]
    arrived = lax.ppermute(send, "c", pair)
    held, base, back_near, back_far = local(
        back_kernel,
        "back",
        (half_rows, ((ROWS, WIDTH), f32), rows, rows),
        [scalar] + [whole] * 6,
        8,
        flops=10**9,
    )(core, d_table, d_queries, normed_t, attn_t, scaled, w_qkv)
    half = (held.astype(f32) + arrived.astype(f32)).astype(b16)
    half, base, back_near, back_far = lax.optimization_barrier((half, base, back_near, back_far))
    back_near = swapped(back_near, 0)
    count = lax.axis_size(SPACE)
    middle = count // 2
    ends = [(middle - 1, count - 1), (0, middle)]
    crossed = lax.ppermute(back_far, SPACE, ends + [(b, a) for a, b in ends])
    plane = lax.axis_size(("x", "z"))
    parts = half.reshape(plane, 2 * WIDTH // plane, WIDTH)
    part = total(lax.all_to_all(parts, ("x", "z"), 0, 0, tiled=True))
    part, crossed = lax.optimization_barrier((part, crossed))
    at_end = jnp.logical_or(position == 0, position == count - 1)
    back_far = jnp.where(at_end, crossed, back_far)
    pairs = [(i, i + 1) for i in range(1, count - 1, 2) if i != middle - 1]
    pairs = pairs + [(b, a) for a, b in pairs] + [(count - 1, middle), (0, middle - 1)]
    back_far = lax.ppermute(back_far, SPACE, pairs)
    parts = spread(part, ("yl", "yh"))
    (copies,) = local(gather_kernel, "gather", (((plane,) + part.shape, b16),), [whole], 4)(parts)
    half = lax.all_to_all(copies, ("x", "z"), 0, 0, tiled=True).reshape(2 * WIDTH, WIDTH)
    (grad_input,) = local(input_kernel, "grad_input", (rows,), [whole] * 6, 8, flops=10**10)(
        base, back_near, back_far, values, cot, gains
    )
    half, grad_input = lax.optimization_barrier((half, grad_input))
    other = lax.ppermute(half, "c", pair)

    grad_wqkv, grad_wout, grad_gain = local(
        output_kernel,
        "outputs",
        (((WIDTH, 3 * WIDTH), f32), ((WIDTH, WIDTH), f32), ((WIDTH,), f32)),
        [scalar] + [whole] * 4,
        8,
        moved=4 * 10**6,
    )(core, half, other, w_qkv, gain)
    return (grad_input[None], grad_wqkv, grad_wout, grad_gain)


def solution(mesh):
    fine = Mesh(mesh.devices.reshape(4, 2, 2, 4, 8), ("yl", "c", "yh", "x", "z"))
    region = ("yl", "c")
    split = P(region, SPACE, None)
    return jax.shard_map(
        shards,
        mesh=fine,
        in_specs=(split, split, split, P(region, SPACE), P(), P(), P()),
        out_specs=(split, P(), P(), P()),
        check_vma=False,
    )
```

```python
import math

import jax
import jax.numpy as jnp
import numpy as np
from jax import lax
from jax.experimental import pallas as pl
from jax.experimental.pallas import tpu as pltpu
from jax.sharding import Mesh
from jax.sharding import PartitionSpec as P

HEADS = 6
SIDE = 9
ROWS = 288
WIDTH = 384
HEAD = 64
KEYS = 896
SPACE = ("yh", "x", "z")
HIDDEN = -1e30


def inner(left, right):
    return lax.dot_general(
        left, right, (((1,), (1,)), ((), ())), preferred_element_type=jnp.float32
    )


def dot(left, right):
    return jnp.dot(left, right, preferred_element_type=jnp.float32)


def swapped(block, first):
    count = lax.axis_size(SPACE)
    pairs = [(i, i + 1) for i in range(first, count - 1, 2)]
    return lax.ppermute(block, SPACE, pairs + [(b, a) for a, b in pairs])


AXES = ("yl", "c", "yh", "x", "z")
SIZES = (4, 2, 2, 4, 8)
GRID = np.arange(math.prod(SIZES)).reshape(SIZES)
PLANES = [GRID[i, 0, j].ravel().tolist() for i in range(4) for j in range(2)]
PLANES += [GRID[:, 1, :, :, k].ravel().tolist() for k in range(8)]
RINGS = [GRID[:, 0, :, i, k].ravel().tolist() for i in range(4) for k in range(8)]
RINGS += [GRID[i, 1, j, k].ravel().tolist() for i in range(4) for j in range(2) for k in range(4)]


def exchanged(parts, groups):
    return lax.all_to_all(parts, AXES, 0, 0, axis_index_groups=groups, tiled=True)


def total(parts):
    return jnp.sum(parts.astype(jnp.float32), axis=0).astype(jnp.bfloat16)


def unit_rows(values, gain):
    power = jnp.mean(values * values, axis=1, keepdims=True)
    return values * lax.rsqrt(power + 1e-06) * gain


def fetch(pairs, sems):
    copies = [
        pltpu.make_async_copy(source, target, sems.at[i]) for i, (source, target) in enumerate(pairs)
    ]
    for copy in copies:
        copy.start()
    return copies


def prepare_kernel(
    alive, tokens_in, cot_in, gain, wqkv_in, wout_in, own, kv, q8, q8t, g, scaled,
    tokens, cot, wqkv, wout, sems,
):
    copies = fetch([(tokens_in, tokens), (wqkv_in, wqkv), (cot_in, cot), (wout_in, wout)], sems)
    copies[0].wait()
    own[...] = unit_rows(tokens[...].astype(jnp.float32), gain[...]).astype(jnp.bfloat16)
    copies[1].wait()
    queries = dot(own[...], wqkv[:, 0:WIDTH]).astype(jnp.bfloat16).astype(jnp.float32)
    eighth = (queries * (1.0 / math.sqrt(HEAD))).astype(jnp.bfloat16)
    q8[...] = eighth
    q8t[...] = eighth.T
    kv[...] = dot(own[...], wqkv[:, WIDTH:]).astype(jnp.bfloat16)
    copies[2].wait()
    block = ROWS // SIDE
    for at in range(SIDE):
        rows = slice(at * block, at * block + block)
        part = cot[rows].astype(jnp.float32) * alive[at].astype(jnp.float32)
        scaled[rows] = part.astype(jnp.bfloat16)
    copies[3].wait()
    g[...] = inner(scaled[...], wout[...]).astype(jnp.bfloat16)


def attention_kernel(
    core, far, near, own, kv, q8, q8t, g, scaled, fq, fk, gain, wqkv,
    send, dt, dq, normed_t, attn_t, normed, table, scores, expo, dshare, dscores,
):
    normed[0:ROWS] = own[...]
    normed[3 * ROWS : KEYS] = jnp.zeros((KEYS - 3 * ROWS, WIDTH), jnp.bfloat16)
    table[0:ROWS] = kv[...]
    table[3 * ROWS : KEYS] = jnp.zeros((KEYS - 3 * ROWS, 2 * WIDTH), jnp.bfloat16)
    for side, halo in enumerate((near, far)):
        rows = slice((side + 1) * ROWS, (side + 2) * ROWS)
        unit = unit_rows(halo[...].astype(jnp.float32), gain[...]).astype(jnp.bfloat16)
        normed[rows] = unit
        table[rows] = dot(unit, wqkv[:, WIDTH:]).astype(jnp.bfloat16)
    normed_t[...] = normed[...].T
    both = lax.broadcasted_iota(jnp.int32, (2 * ROWS, 128), 0) < ROWS
    low = lax.broadcasted_iota(jnp.int32, (2 * ROWS, 128), 1) < HEAD
    keep = both == low
    zero = jnp.zeros((2 * ROWS, 128), jnp.float32)
    chunks = [slice(at, at + 32) for at in range(0, 2 * ROWS, 32)]
    pairs = range(HEADS // 2)
    lanes = [slice(pair * 128, pair * 128 + 128) for pair in pairs]
    values = [slice(WIDTH + at.start, WIDTH + at.stop) for at in lanes]
    shares, results, grads, deltas = [], [], [], []

    def twice(block):
        return jnp.concatenate([block, block], axis=0).astype(jnp.float32)

    def joined(block):
        return jnp.where(low[:ROWS], block[:ROWS], block[ROWS:]).astype(jnp.bfloat16)

    for pair in pairs:
        queries = jnp.where(keep, twice(q8[:, lanes[pair]]), zero).astype(jnp.bfloat16)
        queries = jnp.concatenate([queries, jnp.concatenate([fq[...], fq[...]], axis=0)], axis=1)
        scores[pair] = inner(queries, jnp.concatenate([table[:, lanes[pair]], fk[...]], axis=1))
    for pair in pairs:
        share = []
        for rows in chunks:
            block = scores[pair, rows]
            block = jnp.exp(block - jnp.max(block, axis=1, keepdims=True))
            share.append(1.0 / jnp.sum(block, axis=1, keepdims=True))
            expo[pair, rows] = block.astype(jnp.bfloat16)
        shares.append(jnp.concatenate(share, axis=0))
    for pair in pairs:
        results.append(dot(expo[pair], table[:, values[pair]]) * shares[pair])
        grad = jnp.where(keep, twice(g[:, lanes[pair]]) * shares[pair], zero)
        grads.append(grad.astype(jnp.bfloat16))
        dshare[pair] = inner(grads[pair], table[:, values[pair]])
        delta = grads[pair].astype(jnp.float32) * results[pair]
        deltas.append(jnp.sum(delta, axis=1, keepdims=True))
    for pair in pairs:
        for rows in chunks:
                block = (dshare[pair, rows] - deltas[pair][rows]).astype(jnp.bfloat16)
                dscores[pair, rows] = expo[pair, rows] * block
    for pair in pairs:
        moved = dot(dscores[pair], table[:, lanes[pair]]) * (1.0 / math.sqrt(HEAD))
        dq[:, lanes[pair]] = joined(moved)
        attn_t[lanes[pair]] = joined(results[pair]).T
        turned = (grads[pair][:ROWS] + grads[pair][ROWS:]).T
        for half in range(2):
            rows = slice(half * ROWS, half * ROWS + ROWS)
            at = (2 * pair + half) * HEAD
            part = q8t[at : at + HEAD]
            dt[at : at + HEAD] = dot(part, dscores[pair, rows]).astype(jnp.bfloat16)
            part = turned[half * HEAD : half * HEAD + HEAD]
            at += WIDTH
            dt[at : at + HEAD] = dot(part, expo[pair, rows]).astype(jnp.bfloat16)

    @pl.when(core[0] == 0)
    def _():
        value_half(send, normed_t, dt, attn_t, scaled)

    @pl.when(core[0] == 1)
    def _():
        key_half(send, normed_t, dt, dq)


def key_half(out, normed_t, dt, dq):
    out[0:WIDTH] = dot(normed_t[:, 0:ROWS], dq[...]).astype(jnp.bfloat16)
    out[WIDTH:] = inner(normed_t[...], dt[0:WIDTH]).astype(jnp.bfloat16)


def value_half(out, normed_t, dt, attn_t, scaled):
    out[0:WIDTH] = inner(normed_t[...], dt[WIDTH:]).astype(jnp.bfloat16)
    out[WIDTH:] = dot(attn_t[...], scaled[...]).astype(jnp.bfloat16)


def back_kernel(core, dt, dq, normed_t, attn_t, scaled, wqkv, held, base, near, far):
    back = lax.dot_general(
        dt[...], wqkv[:, WIDTH:], (((0,), (1,)), ((), ())), preferred_element_type=jnp.float32
    )
    near[...] = back[ROWS : 2 * ROWS].astype(jnp.bfloat16)
    far[...] = back[2 * ROWS : 3 * ROWS].astype(jnp.bfloat16)
    base[...] = back[0:ROWS] + inner(dq[...], wqkv[:, 0:WIDTH])

    @pl.when(core[0] == 0)
    def _():
        key_half(held, normed_t, dt, dq)

    @pl.when(core[0] == 1)
    def _():
        value_half(held, normed_t, dt, attn_t, scaled)


def gather_kernel(parts, copies):
    part = jnp.sum(parts[...].astype(jnp.float32), axis=0).astype(jnp.bfloat16)
    copies[...] = jnp.broadcast_to(part[None], copies.shape)


def input_kernel(base, near, far, tokens, cot, gain, grad_input):
    d_normed = base[...] + near[...].astype(jnp.float32) + far[...].astype(jnp.float32)
    inward = d_normed.astype(jnp.bfloat16).astype(jnp.float32) * gain[...]
    values = tokens[...].astype(jnp.float32)
    root = lax.rsqrt(jnp.mean(values * values, axis=1, keepdims=True) + 1e-06)
    slope = jnp.mean(inward * values, axis=1, keepdims=True) * root * root
    moved = cot[...].astype(jnp.float32) + root * (inward - values * slope)
    grad_input[...] = moved.astype(jnp.bfloat16)


def output_kernel(core, mine, other, wqkv, gain, grad_qkv, grad_out, grad_gain):
    scale = 1.0 / math.sqrt(512 * ROWS)
    me = core[0]

    def halves(first, second):
        query = first[0:WIDTH].astype(jnp.float32) * scale
        key = first[WIDTH:].astype(jnp.float32) * scale
        value = second[0:WIDTH].astype(jnp.float32) * scale
        grad_qkv[:, 0:WIDTH] = query
        grad_qkv[:, WIDTH : 2 * WIDTH] = key
        grad_qkv[:, 2 * WIDTH :] = value
        grad_out[...] = second[WIDTH:].astype(jnp.float32) * scale
        moved = query * wqkv[:, 0:WIDTH].astype(jnp.float32)
        moved += key * wqkv[:, WIDTH : 2 * WIDTH].astype(jnp.float32)
        moved += value * wqkv[:, 2 * WIDTH :].astype(jnp.float32)
        grad_gain[...] = jnp.sum(moved.T, axis=0) / gain[...]

    @pl.when(me == 0)
    def _():
        halves(mine, other)

    @pl.when(me == 1)
    def _():
        halves(other, mine)


def local(body, name, shapes, in_specs, vmem, scratch=(), flops=10**8, moved=10**6):
    return pl.pallas_call(
        body,
        out_shape=tuple(jax.ShapeDtypeStruct(shape, kind) for shape, kind in shapes),
        in_specs=in_specs,
        out_specs=(pl.BlockSpec(memory_space=pltpu.VMEM),) * len(shapes),
        scratch_shapes=scratch,
        compiler_params=pltpu.CompilerParams(vmem_limit_bytes=vmem * 2**20),
        cost_estimate=pl.CostEstimate(flops=flops, bytes_accessed=moved, transcendentals=0),
        name=name,
    )


def shards(tokens, cotangent, neighbours, active, gain, w_qkv, w_out):
    values = tokens[0]
    cot = cotangent[0]
    lists = neighbours[0]
    block = ROWS // SIDE
    position = lax.axis_index(SPACE)
    core = jnp.reshape(lax.axis_index("c"), (1,)).astype(jnp.int32)
    near = swapped(values, 0)
    far = swapped(values, 1)
    gains = gain[None]

    b16, f32 = jnp.bfloat16, jnp.float32
    whole = pl.BlockSpec(memory_space=pltpu.VMEM)
    scalar = pl.BlockSpec(memory_space=pltpu.SMEM)
    outside = pl.BlockSpec(memory_space=pltpu.HBM)
    rows = ((ROWS, WIDTH), b16)
    half_rows = ((2 * WIDTH, WIDTH), b16)
    dma = pltpu.SemaphoreType.DMA
    own, kv, q8, q8t, g, scaled = local(
        prepare_kernel,
        "prepare",
        (rows, ((ROWS, 2 * WIDTH), b16), rows, ((WIDTH, ROWS), b16), rows, rows),
        [scalar, outside, outside, whole, outside, outside],
        8,
        (
            pltpu.VMEM((ROWS, WIDTH), b16),
            pltpu.VMEM((ROWS, WIDTH), b16),
            pltpu.VMEM((WIDTH, 3 * WIDTH), b16),
            pltpu.VMEM((WIDTH, WIDTH), b16),
            dma((4,)),
        ),
        flops=4 * 10**8,
    )(active[0], values, cot, gains, w_qkv, w_out)

    parity = position % 2
    slabs = jnp.stack([position, position + 1 - 2 * parity, position - 1 + 2 * parity])
    ids = (slabs[:, None] * SIDE + jnp.arange(SIDE)[None, :]).reshape(-1)
    seen = jnp.any((lists[:, :, None] == ids) & (lists[:, :, None] >= 0), axis=1)
    hidden = jnp.where(seen, 0.0, HIDDEN).T.astype(b16)
    fk = jnp.repeat(hidden, block, axis=0)
    fk = jnp.pad(fk, ((0, KEYS - 3 * ROWS), (0, 0)), constant_values=HIDDEN)
    fk = jnp.pad(fk, ((0, 0), (0, 128 - SIDE)))
    row_block = lax.broadcasted_iota(jnp.int32, (ROWS, 128), 0) // block
    fq = (row_block == lax.broadcasted_iota(jnp.int32, (ROWS, 128), 1)).astype(b16)

    pair_rows = (HEADS // 2, 2 * ROWS, KEYS)
    send, d_table, d_queries, normed_t, attn_t = local(
        attention_kernel,
        "attention",
        (half_rows, ((2 * WIDTH, KEYS), b16), rows, ((WIDTH, KEYS), b16), ((WIDTH, ROWS), b16)),
        [scalar] + [whole] * 12,
        32,
        (
            pltpu.VMEM((KEYS, WIDTH), b16),
            pltpu.VMEM((KEYS, 2 * WIDTH), b16),
            pltpu.VMEM(pair_rows, f32),
            pltpu.VMEM(pair_rows, b16),
            pltpu.VMEM(pair_rows, f32),
            pltpu.VMEM(pair_rows, b16),
        ),
        flops=3 * 10**9,
        moved=4 * 10**6,
    )(core, far, near, own, kv, q8, q8t, g, scaled, fq, fk, gains, w_qkv)

    pair = [(0, 1), (1, 0)]
    arrived = lax.ppermute(send, "c", pair)
    held, base, back_near, back_far = local(
        back_kernel,
        "back",
        (half_rows, ((ROWS, WIDTH), f32), rows, rows),
        [scalar] + [whole] * 6,
        8,
        flops=10**9,
    )(core, d_table, d_queries, normed_t, attn_t, scaled, w_qkv)
    half = (held.astype(f32) + arrived.astype(f32)).astype(b16)
    half, base, back_near, back_far = lax.optimization_barrier((half, base, back_near, back_far))
    back_near = swapped(back_near, 0)
    count = lax.axis_size(SPACE)
    middle = count // 2
    pairs = [(i, i + 1) for i in range(1, count - 1, 2) if i != middle - 1]
    pairs = pairs + [(b, a) for a, b in pairs] + [(middle - 1, 0), (middle, count - 1)]
    moved = lax.ppermute(back_far, SPACE, pairs)
    plane, ring = len(PLANES[0]), len(RINGS[0])
    parts = half.reshape(plane, 2 * WIDTH // plane, WIDTH)
    part = total(exchanged(parts, PLANES))
    part, moved = lax.optimization_barrier((part, moved))
    crossed = lax.ppermute(moved, SPACE, [(0, middle), (count - 1, middle - 1)])
    inside = jnp.logical_and(position > 0, position < count - 1)
    in_middle = jnp.logical_or(position == middle - 1, position == middle)
    back_far = jnp.where(in_middle, crossed, jnp.where(inside, moved, jnp.zeros_like(moved)))
    parts = exchanged(jnp.broadcast_to(part[None], (ring,) + part.shape), RINGS)
    (copies,) = local(gather_kernel, "gather", (((plane,) + part.shape, b16),), [whole], 4)(parts)
    half = exchanged(copies, PLANES).reshape(2 * WIDTH, WIDTH)
    (grad_input,) = local(input_kernel, "grad_input", (rows,), [whole] * 6, 8, flops=10**10)(
        base, back_near, back_far, values, cot, gains
    )
    half, grad_input = lax.optimization_barrier((half, grad_input))
    other = lax.ppermute(half, "c", pair)

    grad_wqkv, grad_wout, grad_gain = local(
        output_kernel,
        "outputs",
        (((WIDTH, 3 * WIDTH), f32), ((WIDTH, WIDTH), f32), ((WIDTH,), f32)),
        [scalar] + [whole] * 4,
        8,
        moved=4 * 10**6,
    )(core, half, other, w_qkv, gain)
    return (grad_input[None], grad_wqkv, grad_wout, grad_gain)


def solution(mesh):
    fine = Mesh(mesh.devices.reshape(SIZES), AXES)
    region = ("yl", "c")
    split = P(region, SPACE, None)
    return jax.shard_map(
        shards,
        mesh=fine,
        in_specs=(split, split, split, P(region, SPACE), P(), P(), P()),
        out_specs=(split, P(), P(), P()),
        check_vma=False,
    )
```

```python
import math

import jax
import jax.numpy as jnp
import numpy as np
from jax import lax
from jax.experimental import pallas as pl
from jax.experimental.pallas import tpu as pltpu
from jax.sharding import Mesh
from jax.sharding import PartitionSpec as P

HEADS = 6
SIDE = 9
ROWS = 288
WIDTH = 384
HEAD = 64
KEYS = 896
SPACE = ("yh", "x", "z")
HIDDEN = -1e30


def inner(left, right):
    return lax.dot_general(
        left, right, (((1,), (1,)), ((), ())), preferred_element_type=jnp.float32
    )


def dot(left, right):
    return jnp.dot(left, right, preferred_element_type=jnp.float32)


def swapped(block, first):
    count = lax.axis_size(SPACE)
    pairs = [(i, i + 1) for i in range(first, count - 1, 2)]
    return lax.ppermute(block, SPACE, pairs + [(b, a) for a, b in pairs])


AXES = ("yl", "c", "yh", "x", "z")
SIZES = (4, 2, 2, 4, 8)
GRID = np.arange(math.prod(SIZES)).reshape(SIZES)
PLANES = [GRID[i, 0, j].ravel().tolist() for i in range(4) for j in range(2)]
PLANES += [GRID[:, 1, :, :, k].ravel().tolist() for k in range(8)]
RINGS = [GRID[:, 0, :, i, k].ravel().tolist() for i in range(4) for k in range(8)]
RINGS += [GRID[i, 1, j, k].ravel().tolist() for i in range(4) for j in range(2) for k in range(4)]


def exchanged(parts, groups):
    return lax.all_to_all(parts, AXES, 0, 0, axis_index_groups=groups, tiled=True)


def total(parts):
    return jnp.sum(parts.astype(jnp.float32), axis=0).astype(jnp.bfloat16)


def unit_rows(values, gain):
    power = jnp.mean(values * values, axis=1, keepdims=True)
    return values * lax.rsqrt(power + 1e-06) * gain


def fetch(pairs, sems):
    copies = [
        pltpu.make_async_copy(source, target, sems.at[i]) for i, (source, target) in enumerate(pairs)
    ]
    for copy in copies:
        copy.start()
    return copies


def prepare_kernel(
    alive, tokens_in, cot_in, gain, wqkv_in, wout_in, own, kv, q8, q8t, g, scaled,
    tokens, cot, wqkv, wout, sems,
):
    copies = fetch([(tokens_in, tokens), (wqkv_in, wqkv), (cot_in, cot), (wout_in, wout)], sems)
    copies[0].wait()
    own[...] = unit_rows(tokens[...].astype(jnp.float32), gain[...]).astype(jnp.bfloat16)
    copies[1].wait()
    queries = dot(own[...], wqkv[:, 0:WIDTH]).astype(jnp.bfloat16).astype(jnp.float32)
    eighth = (queries * (1.0 / math.sqrt(HEAD))).astype(jnp.bfloat16)
    q8[...] = eighth
    q8t[...] = eighth.T
    kv[...] = dot(own[...], wqkv[:, WIDTH:]).astype(jnp.bfloat16)
    copies[2].wait()
    block = ROWS // SIDE
    for at in range(SIDE):
        rows = slice(at * block, at * block + block)
        part = cot[rows].astype(jnp.float32) * alive[at].astype(jnp.float32)
        scaled[rows] = part.astype(jnp.bfloat16)
    copies[3].wait()
    g[...] = inner(scaled[...], wout[...]).astype(jnp.bfloat16)


def attention_kernel(
    core, near, far, own, kv, q8, q8t, g, scaled, fq, fk, gain, wqkv,
    send, dt, dq, normed_t, attn_t, normed, table, scores, expo, dshare, dscores,
):
    normed[0:ROWS] = own[...]
    normed[3 * ROWS : KEYS] = jnp.zeros((KEYS - 3 * ROWS, WIDTH), jnp.bfloat16)
    table[0:ROWS] = kv[...]
    table[3 * ROWS : KEYS] = jnp.zeros((KEYS - 3 * ROWS, 2 * WIDTH), jnp.bfloat16)
    for side, halo in enumerate((near, far)):
        rows = slice((side + 1) * ROWS, (side + 2) * ROWS)
        unit = unit_rows(halo[...].astype(jnp.float32), gain[...]).astype(jnp.bfloat16)
        normed[rows] = unit
        table[rows] = dot(unit, wqkv[:, WIDTH:]).astype(jnp.bfloat16)
    normed_t[...] = normed[...].T
    both = lax.broadcasted_iota(jnp.int32, (2 * ROWS, 128), 0) < ROWS
    low = lax.broadcasted_iota(jnp.int32, (2 * ROWS, 128), 1) < HEAD
    keep = both == low
    zero = jnp.zeros((2 * ROWS, 128), jnp.float32)
    chunks = [slice(at, at + 32) for at in range(0, 2 * ROWS, 32)]
    pairs = range(HEADS // 2)
    lanes = [slice(pair * 128, pair * 128 + 128) for pair in pairs]
    values = [slice(WIDTH + at.start, WIDTH + at.stop) for at in lanes]
    shares, results, grads, deltas = [], [], [], []

    def twice(block):
        return jnp.concatenate([block, block], axis=0).astype(jnp.float32)

    def joined(block):
        return jnp.where(low[:ROWS], block[:ROWS], block[ROWS:]).astype(jnp.bfloat16)

    for pair in pairs:
        queries = jnp.where(keep, twice(q8[:, lanes[pair]]), zero).astype(jnp.bfloat16)
        queries = jnp.concatenate([queries, jnp.concatenate([fq[...], fq[...]], axis=0)], axis=1)
        scores[pair] = inner(queries, jnp.concatenate([table[:, lanes[pair]], fk[...]], axis=1))
    for pair in pairs:
        share = []
        for rows in chunks:
            block = scores[pair, rows]
            block = jnp.exp(block - jnp.max(block, axis=1, keepdims=True))
            share.append(1.0 / jnp.sum(block, axis=1, keepdims=True))
            expo[pair, rows] = block.astype(jnp.bfloat16)
        shares.append(jnp.concatenate(share, axis=0))
    for pair in pairs:
        results.append(dot(expo[pair], table[:, values[pair]]) * shares[pair])
        grad = jnp.where(keep, twice(g[:, lanes[pair]]) * shares[pair], zero)
        grads.append(grad.astype(jnp.bfloat16))
        dshare[pair] = inner(grads[pair], table[:, values[pair]])
        delta = grads[pair].astype(jnp.float32) * results[pair]
        deltas.append(jnp.sum(delta, axis=1, keepdims=True))
    for pair in pairs:
        for rows in chunks:
                block = (dshare[pair, rows] - deltas[pair][rows]).astype(jnp.bfloat16)
                dscores[pair, rows] = expo[pair, rows] * block
    for pair in pairs:
        moved = dot(dscores[pair], table[:, lanes[pair]]) * (1.0 / math.sqrt(HEAD))
        dq[:, lanes[pair]] = joined(moved)
        attn_t[lanes[pair]] = joined(results[pair]).T
        turned = (grads[pair][:ROWS] + grads[pair][ROWS:]).T
        for half in range(2):
            rows = slice(half * ROWS, half * ROWS + ROWS)
            at = (2 * pair + half) * HEAD
            part = q8t[at : at + HEAD]
            dt[at : at + HEAD] = dot(part, dscores[pair, rows]).astype(jnp.bfloat16)
            part = turned[half * HEAD : half * HEAD + HEAD]
            at += WIDTH
            dt[at : at + HEAD] = dot(part, expo[pair, rows]).astype(jnp.bfloat16)

    @pl.when(core[0] == 0)
    def _():
        value_half(send, normed_t, dt, attn_t, scaled)

    @pl.when(core[0] == 1)
    def _():
        key_half(send, normed_t, dt, dq)


def key_half(out, normed_t, dt, dq):
    out[0:WIDTH] = dot(normed_t[:, 0:ROWS], dq[...]).astype(jnp.bfloat16)
    out[WIDTH:] = inner(normed_t[...], dt[0:WIDTH]).astype(jnp.bfloat16)


def value_half(out, normed_t, dt, attn_t, scaled):
    out[0:WIDTH] = inner(normed_t[...], dt[WIDTH:]).astype(jnp.bfloat16)
    out[WIDTH:] = dot(attn_t[...], scaled[...]).astype(jnp.bfloat16)


def back_kernel(core, dt, dq, normed_t, attn_t, scaled, wqkv, held, base, near, far):
    back = lax.dot_general(
        dt[...], wqkv[:, WIDTH:], (((0,), (1,)), ((), ())), preferred_element_type=jnp.float32
    )
    near[...] = back[ROWS : 2 * ROWS].astype(jnp.bfloat16)
    far[...] = back[2 * ROWS : 3 * ROWS].astype(jnp.bfloat16)
    base[...] = back[0:ROWS] + inner(dq[...], wqkv[:, 0:WIDTH])

    @pl.when(core[0] == 0)
    def _():
        key_half(held, normed_t, dt, dq)

    @pl.when(core[0] == 1)
    def _():
        value_half(held, normed_t, dt, attn_t, scaled)


def gather_kernel(parts, copies):
    part = jnp.sum(parts[...].astype(jnp.float32), axis=0).astype(jnp.bfloat16)
    copies[...] = jnp.broadcast_to(part[None], copies.shape)


def input_kernel(base, near, far, tokens, cot, gain, grad_input):
    d_normed = base[...] + near[...].astype(jnp.float32) + far[...].astype(jnp.float32)
    inward = d_normed.astype(jnp.bfloat16).astype(jnp.float32) * gain[...]
    values = tokens[...].astype(jnp.float32)
    root = lax.rsqrt(jnp.mean(values * values, axis=1, keepdims=True) + 1e-06)
    slope = jnp.mean(inward * values, axis=1, keepdims=True) * root * root
    moved = cot[...].astype(jnp.float32) + root * (inward - values * slope)
    grad_input[...] = moved.astype(jnp.bfloat16)


def output_kernel(core, mine, other, wqkv, gain, grad_qkv, grad_out, grad_gain):
    scale = 1.0 / math.sqrt(512 * ROWS)
    me = core[0]

    def halves(first, second):
        query = first[0:WIDTH].astype(jnp.float32) * scale
        key = first[WIDTH:].astype(jnp.float32) * scale
        value = second[0:WIDTH].astype(jnp.float32) * scale
        grad_qkv[:, 0:WIDTH] = query
        grad_qkv[:, WIDTH : 2 * WIDTH] = key
        grad_qkv[:, 2 * WIDTH :] = value
        grad_out[...] = second[WIDTH:].astype(jnp.float32) * scale
        moved = query * wqkv[:, 0:WIDTH].astype(jnp.float32)
        moved += key * wqkv[:, WIDTH : 2 * WIDTH].astype(jnp.float32)
        moved += value * wqkv[:, 2 * WIDTH :].astype(jnp.float32)
        grad_gain[...] = jnp.sum(moved.T, axis=0) / gain[...]

    @pl.when(me == 0)
    def _():
        halves(mine, other)

    @pl.when(me == 1)
    def _():
        halves(other, mine)


def local(body, name, shapes, in_specs, vmem, scratch=(), flops=10**8, moved=10**6):
    return pl.pallas_call(
        body,
        out_shape=tuple(jax.ShapeDtypeStruct(shape, kind) for shape, kind in shapes),
        in_specs=in_specs,
        out_specs=(pl.BlockSpec(memory_space=pltpu.VMEM),) * len(shapes),
        scratch_shapes=scratch,
        compiler_params=pltpu.CompilerParams(vmem_limit_bytes=vmem * 2**20),
        cost_estimate=pl.CostEstimate(flops=flops, bytes_accessed=moved, transcendentals=0),
        name=name,
    )


def shards(tokens, cotangent, neighbours, active, gain, w_qkv, w_out):
    values = tokens[0]
    cot = cotangent[0]
    lists = neighbours[0]
    block = ROWS // SIDE
    position = lax.axis_index(SPACE)
    core = jnp.reshape(lax.axis_index("c"), (1,)).astype(jnp.int32)
    near = swapped(values, 0)
    far = swapped(values, 1)
    gains = gain[None]

    b16, f32 = jnp.bfloat16, jnp.float32
    whole = pl.BlockSpec(memory_space=pltpu.VMEM)
    scalar = pl.BlockSpec(memory_space=pltpu.SMEM)
    outside = pl.BlockSpec(memory_space=pltpu.HBM)
    rows = ((ROWS, WIDTH), b16)
    half_rows = ((2 * WIDTH, WIDTH), b16)
    dma = pltpu.SemaphoreType.DMA
    own, kv, q8, q8t, g, scaled = local(
        prepare_kernel,
        "prepare",
        (rows, ((ROWS, 2 * WIDTH), b16), rows, ((WIDTH, ROWS), b16), rows, rows),
        [scalar, outside, outside, whole, outside, outside],
        8,
        (
            pltpu.VMEM((ROWS, WIDTH), b16),
            pltpu.VMEM((ROWS, WIDTH), b16),
            pltpu.VMEM((WIDTH, 3 * WIDTH), b16),
            pltpu.VMEM((WIDTH, WIDTH), b16),
            dma((4,)),
        ),
        flops=4 * 10**8,
    )(active[0], values, cot, gains, w_qkv, w_out)

    parity = position % 2
    slabs = jnp.stack([position, position + 1 - 2 * parity, position - 1 + 2 * parity])
    ids = (slabs[:, None] * SIDE + jnp.arange(SIDE)[None, :]).reshape(-1)
    seen = jnp.any((lists[:, :, None] == ids) & (lists[:, :, None] >= 0), axis=1)
    hidden = jnp.where(seen, 0.0, HIDDEN).T.astype(b16)
    fk = jnp.repeat(hidden, block, axis=0)
    fk = jnp.pad(fk, ((0, KEYS - 3 * ROWS), (0, 0)), constant_values=HIDDEN)
    fk = jnp.pad(fk, ((0, 0), (0, 128 - SIDE)))
    row_block = lax.broadcasted_iota(jnp.int32, (ROWS, 128), 0) // block
    fq = (row_block == lax.broadcasted_iota(jnp.int32, (ROWS, 128), 1)).astype(b16)

    pair_rows = (HEADS // 2, 2 * ROWS, KEYS)
    send, d_table, d_queries, normed_t, attn_t = local(
        attention_kernel,
        "attention",
        (half_rows, ((2 * WIDTH, KEYS), b16), rows, ((WIDTH, KEYS), b16), ((WIDTH, ROWS), b16)),
        [scalar] + [whole] * 12,
        32,
        (
            pltpu.VMEM((KEYS, WIDTH), b16),
            pltpu.VMEM((KEYS, 2 * WIDTH), b16),
            pltpu.VMEM(pair_rows, f32),
            pltpu.VMEM(pair_rows, b16),
            pltpu.VMEM(pair_rows, f32),
            pltpu.VMEM(pair_rows, b16),
        ),
        flops=3 * 10**9,
        moved=4 * 10**6,
    )(core, near, far, own, kv, q8, q8t, g, scaled, fq, fk, gains, w_qkv)

    pair = [(0, 1), (1, 0)]
    arrived = lax.ppermute(send, "c", pair)
    held, base, back_near, back_far = local(
        back_kernel,
        "back",
        (half_rows, ((ROWS, WIDTH), f32), rows, rows),
        [scalar] + [whole] * 6,
        8,
        flops=10**9,
    )(core, d_table, d_queries, normed_t, attn_t, scaled, w_qkv)
    half = (held.astype(f32) + arrived.astype(f32)).astype(b16)
    half, base, back_near, back_far = lax.optimization_barrier((half, base, back_near, back_far))
    back_near = swapped(back_near, 0)
    count = lax.axis_size(SPACE)
    middle = count // 2
    moved = lax.ppermute(back_far, SPACE, [(middle - 1, 0), (middle, count - 1)])
    plane, ring = len(PLANES[0]), len(RINGS[0])
    parts = half.reshape(plane, 2 * WIDTH // plane, WIDTH)
    part = total(exchanged(parts, PLANES))
    at_end = jnp.logical_or(position == 0, position == count - 1)
    pairs = [(i, i + 1) for i in range(1, count - 1, 2) if i != middle - 1]
    pairs = pairs + [(b, a) for a, b in pairs] + [(0, middle), (count - 1, middle - 1)]
    back_far = lax.ppermute(jnp.where(at_end, moved, back_far), SPACE, pairs)
    parts = exchanged(jnp.broadcast_to(part[None], (ring,) + part.shape), RINGS)
    (copies,) = local(gather_kernel, "gather", (((plane,) + part.shape, b16),), [whole], 4)(parts)
    half = exchanged(copies, PLANES).reshape(2 * WIDTH, WIDTH)
    (grad_input,) = local(input_kernel, "grad_input", (rows,), [whole] * 6, 8, flops=10**10)(
        base, back_near, back_far, values, cot, gains
    )
    half, grad_input = lax.optimization_barrier((half, grad_input))
    other = lax.ppermute(half, "c", pair)

    grad_wqkv, grad_wout, grad_gain = local(
        output_kernel,
        "outputs",
        (((WIDTH, 3 * WIDTH), f32), ((WIDTH, WIDTH), f32), ((WIDTH,), f32)),
        [scalar] + [whole] * 4,
        8,
        moved=4 * 10**6,
    )(core, half, other, w_qkv, gain)
    return (grad_input[None], grad_wqkv, grad_wout, grad_gain)


def solution(mesh):
    fine = Mesh(mesh.devices.reshape(SIZES), AXES)
    region = ("yl", "c")
    split = P(region, SPACE, None)
    return jax.shard_map(
        shards,
        mesh=fine,
        in_specs=(split, split, split, P(region, SPACE), P(), P(), P()),
        out_specs=(split, P(), P(), P()),
        check_vma=False,
    )
```

```python
import math

import jax
import jax.numpy as jnp
import numpy as np
from jax import lax
from jax.experimental import pallas as pl
from jax.experimental.pallas import tpu as pltpu
from jax.sharding import Mesh
from jax.sharding import PartitionSpec as P

HEADS = 6
SIDE = 9
ROWS = 288
WIDTH = 384
HEAD = 64
KEYS = 896
SPACE = ("yh", "x", "z")
HIDDEN = -1e30


def inner(left, right):
    return lax.dot_general(
        left, right, (((1,), (1,)), ((), ())), preferred_element_type=jnp.float32
    )


def dot(left, right):
    return jnp.dot(left, right, preferred_element_type=jnp.float32)


def swapped(block, first):
    count = lax.axis_size(SPACE)
    pairs = [(i, i + 1) for i in range(first, count - 1, 2)]
    return lax.ppermute(block, SPACE, pairs + [(b, a) for a, b in pairs])


AXES = ("yl", "c", "yh", "x", "z")
SIZES = (4, 2, 2, 4, 8)
GRID = np.arange(math.prod(SIZES)).reshape(SIZES)
PLANES = [GRID[i, 0, j].ravel().tolist() for i in range(4) for j in range(2)]
PLANES += [GRID[:, 1, :, :, k].ravel().tolist() for k in range(8)]
RINGS = [GRID[:, 0, :, i, k].ravel().tolist() for i in range(4) for k in range(8)]
RINGS += [GRID[i, 1, j, k].ravel().tolist() for i in range(4) for j in range(2) for k in range(4)]


def exchanged(parts, groups):
    return lax.all_to_all(parts, AXES, 0, 0, axis_index_groups=groups, tiled=True)


def total(parts):
    return jnp.sum(parts.astype(jnp.float32), axis=0).astype(jnp.bfloat16)


def unit_rows(values, gain):
    power = jnp.mean(values * values, axis=1, keepdims=True)
    return values * lax.rsqrt(power + 1e-06) * gain


def fetch(pairs, sems):
    copies = [
        pltpu.make_async_copy(source, target, sems.at[i]) for i, (source, target) in enumerate(pairs)
    ]
    for copy in copies:
        copy.start()
    return copies


def prepare_kernel(
    alive, tokens_in, cot_in, gain, wqkv_in, wout_in, own, kv, q8, q8t, g, scaled,
    tokens, cot, wqkv, wout, sems,
):
    copies = fetch([(tokens_in, tokens), (wqkv_in, wqkv), (cot_in, cot), (wout_in, wout)], sems)
    copies[0].wait()
    own[...] = unit_rows(tokens[...].astype(jnp.float32), gain[...]).astype(jnp.bfloat16)
    copies[1].wait()
    queries = dot(own[...], wqkv[:, 0:WIDTH]).astype(jnp.bfloat16).astype(jnp.float32)
    eighth = (queries * (1.0 / math.sqrt(HEAD))).astype(jnp.bfloat16)
    q8[...] = eighth
    q8t[...] = eighth.T
    kv[...] = dot(own[...], wqkv[:, WIDTH:]).astype(jnp.bfloat16)
    copies[2].wait()
    block = ROWS // SIDE
    for at in range(SIDE):
        rows = slice(at * block, at * block + block)
        part = cot[rows].astype(jnp.float32) * alive[at].astype(jnp.float32)
        scaled[rows] = part.astype(jnp.bfloat16)
    copies[3].wait()
    g[...] = inner(scaled[...], wout[...]).astype(jnp.bfloat16)


def attention_kernel(
    core, near, far, own, kv, q8, q8t, g, scaled, fq, fk, gain, wqkv,
    send, dt, dq, normed_t, attn_t, normed, table, scores, expo, dshare, dscores,
):
    normed[0:ROWS] = own[...]
    normed[3 * ROWS : KEYS] = jnp.zeros((KEYS - 3 * ROWS, WIDTH), jnp.bfloat16)
    table[0:ROWS] = kv[...]
    table[3 * ROWS : KEYS] = jnp.zeros((KEYS - 3 * ROWS, 2 * WIDTH), jnp.bfloat16)
    for side, halo in enumerate((near, far)):
        rows = slice((side + 1) * ROWS, (side + 2) * ROWS)
        unit = unit_rows(halo[...].astype(jnp.float32), gain[...]).astype(jnp.bfloat16)
        normed[rows] = unit
        table[rows] = dot(unit, wqkv[:, WIDTH:]).astype(jnp.bfloat16)
    normed_t[...] = normed[...].T
    both = lax.broadcasted_iota(jnp.int32, (2 * ROWS, 128), 0) < ROWS
    low = lax.broadcasted_iota(jnp.int32, (2 * ROWS, 128), 1) < HEAD
    keep = both == low
    zero = jnp.zeros((2 * ROWS, 128), jnp.float32)
    chunks = [slice(at, at + 32) for at in range(0, 2 * ROWS, 32)]
    pairs = range(HEADS // 2)
    lanes = [slice(pair * 128, pair * 128 + 128) for pair in pairs]
    values = [slice(WIDTH + at.start, WIDTH + at.stop) for at in lanes]
    shares, results, grads, deltas = [], [], [], []

    def twice(block):
        return jnp.concatenate([block, block], axis=0).astype(jnp.float32)

    def joined(block):
        return jnp.where(low[:ROWS], block[:ROWS], block[ROWS:]).astype(jnp.bfloat16)

    for pair in pairs:
        queries = jnp.where(keep, twice(q8[:, lanes[pair]]), zero).astype(jnp.bfloat16)
        queries = jnp.concatenate([queries, jnp.concatenate([fq[...], fq[...]], axis=0)], axis=1)
        scores[pair] = inner(queries, jnp.concatenate([table[:, lanes[pair]], fk[...]], axis=1))
    for pair in pairs:
        share = []
        for rows in chunks:
            block = scores[pair, rows]
            block = jnp.exp(block - jnp.max(block, axis=1, keepdims=True))
            share.append(1.0 / jnp.sum(block, axis=1, keepdims=True))
            expo[pair, rows] = block.astype(jnp.bfloat16)
        shares.append(jnp.concatenate(share, axis=0))
    for pair in pairs:
        results.append(dot(expo[pair], table[:, values[pair]]) * shares[pair])
        grad = jnp.where(keep, twice(g[:, lanes[pair]]) * shares[pair], zero)
        grads.append(grad.astype(jnp.bfloat16))
        dshare[pair] = inner(grads[pair], table[:, values[pair]])
        delta = grads[pair].astype(jnp.float32) * results[pair]
        deltas.append(jnp.sum(delta, axis=1, keepdims=True))
    for pair in pairs:
        for rows in chunks:
                block = (dshare[pair, rows] - deltas[pair][rows]).astype(jnp.bfloat16)
                dscores[pair, rows] = expo[pair, rows] * block
    for pair in pairs:
        moved = dot(dscores[pair], table[:, lanes[pair]]) * (1.0 / math.sqrt(HEAD))
        dq[:, lanes[pair]] = joined(moved)
        attn_t[lanes[pair]] = joined(results[pair]).T
        turned = (grads[pair][:ROWS] + grads[pair][ROWS:]).T
        for half in range(2):
            rows = slice(half * ROWS, half * ROWS + ROWS)
            at = (2 * pair + half) * HEAD
            part = q8t[at : at + HEAD]
            dt[at : at + HEAD] = dot(part, dscores[pair, rows]).astype(jnp.bfloat16)
            part = turned[half * HEAD : half * HEAD + HEAD]
            at += WIDTH
            dt[at : at + HEAD] = dot(part, expo[pair, rows]).astype(jnp.bfloat16)

    @pl.when(core[0] == 0)
    def _():
        value_half(send, normed_t, dt, attn_t, scaled)

    @pl.when(core[0] == 1)
    def _():
        key_half(send, normed_t, dt, dq)


def key_half(out, normed_t, dt, dq):
    out[0:WIDTH] = dot(normed_t[:, 0:ROWS], dq[...]).astype(jnp.bfloat16)
    out[WIDTH:] = inner(normed_t[...], dt[0:WIDTH]).astype(jnp.bfloat16)


def value_half(out, normed_t, dt, attn_t, scaled):
    out[0:WIDTH] = inner(normed_t[...], dt[WIDTH:]).astype(jnp.bfloat16)
    out[WIDTH:] = dot(attn_t[...], scaled[...]).astype(jnp.bfloat16)


def back_kernel(core, dt, dq, normed_t, attn_t, scaled, wqkv, held, base, near, far):
    back = lax.dot_general(
        dt[...], wqkv[:, WIDTH:], (((0,), (1,)), ((), ())), preferred_element_type=jnp.float32
    )
    near[...] = back[ROWS : 2 * ROWS].astype(jnp.bfloat16)
    far[...] = back[2 * ROWS : 3 * ROWS].astype(jnp.bfloat16)
    base[...] = back[0:ROWS] + inner(dq[...], wqkv[:, 0:WIDTH])

    @pl.when(core[0] == 0)
    def _():
        key_half(held, normed_t, dt, dq)

    @pl.when(core[0] == 1)
    def _():
        value_half(held, normed_t, dt, attn_t, scaled)


def gather_kernel(parts, copies):
    part = jnp.sum(parts[...].astype(jnp.float32), axis=0).astype(jnp.bfloat16)
    copies[...] = jnp.broadcast_to(part[None], copies.shape)


def input_kernel(base, near, far, tokens, cot, gain, grad_input):
    d_normed = base[...] + near[...].astype(jnp.float32) + far[...].astype(jnp.float32)
    inward = d_normed.astype(jnp.bfloat16).astype(jnp.float32) * gain[...]
    values = tokens[...].astype(jnp.float32)
    root = lax.rsqrt(jnp.mean(values * values, axis=1, keepdims=True) + 1e-06)
    slope = jnp.mean(inward * values, axis=1, keepdims=True) * root * root
    moved = cot[...].astype(jnp.float32) + root * (inward - values * slope)
    grad_input[...] = moved.astype(jnp.bfloat16)


def output_kernel(core, mine, other, wqkv, gain, grad_qkv, grad_out, grad_gain):
    scale = 1.0 / math.sqrt(512 * ROWS)
    me = core[0]

    def halves(first, second):
        query = first[0:WIDTH].astype(jnp.float32) * scale
        key = first[WIDTH:].astype(jnp.float32) * scale
        value = second[0:WIDTH].astype(jnp.float32) * scale
        grad_qkv[:, 0:WIDTH] = query
        grad_qkv[:, WIDTH : 2 * WIDTH] = key
        grad_qkv[:, 2 * WIDTH :] = value
        grad_out[...] = second[WIDTH:].astype(jnp.float32) * scale
        moved = query * wqkv[:, 0:WIDTH].astype(jnp.float32)
        moved += key * wqkv[:, WIDTH : 2 * WIDTH].astype(jnp.float32)
        moved += value * wqkv[:, 2 * WIDTH :].astype(jnp.float32)
        grad_gain[...] = jnp.sum(moved.T, axis=0) / gain[...]

    @pl.when(me == 0)
    def _():
        halves(mine, other)

    @pl.when(me == 1)
    def _():
        halves(other, mine)


def local(body, name, shapes, in_specs, vmem, scratch=(), flops=10**8, moved=10**6):
    return pl.pallas_call(
        body,
        out_shape=tuple(jax.ShapeDtypeStruct(shape, kind) for shape, kind in shapes),
        in_specs=in_specs,
        out_specs=(pl.BlockSpec(memory_space=pltpu.VMEM),) * len(shapes),
        scratch_shapes=scratch,
        compiler_params=pltpu.CompilerParams(vmem_limit_bytes=vmem * 2**20),
        cost_estimate=pl.CostEstimate(flops=flops, bytes_accessed=moved, transcendentals=0),
        name=name,
    )


def shards(tokens, cotangent, neighbours, active, gain, w_qkv, w_out):
    values = tokens[0]
    cot = cotangent[0]
    lists = neighbours[0]
    block = ROWS // SIDE
    position = lax.axis_index(SPACE)
    core = jnp.reshape(lax.axis_index("c"), (1,)).astype(jnp.int32)
    near = swapped(values, 0)
    far = swapped(values, 1)
    gains = gain[None]

    b16, f32 = jnp.bfloat16, jnp.float32
    whole = pl.BlockSpec(memory_space=pltpu.VMEM)
    scalar = pl.BlockSpec(memory_space=pltpu.SMEM)
    outside = pl.BlockSpec(memory_space=pltpu.HBM)
    rows = ((ROWS, WIDTH), b16)
    half_rows = ((2 * WIDTH, WIDTH), b16)
    dma = pltpu.SemaphoreType.DMA
    own, kv, q8, q8t, g, scaled = local(
        prepare_kernel,
        "prepare",
        (rows, ((ROWS, 2 * WIDTH), b16), rows, ((WIDTH, ROWS), b16), rows, rows),
        [scalar, outside, outside, whole, outside, outside],
        8,
        (
            pltpu.VMEM((ROWS, WIDTH), b16),
            pltpu.VMEM((ROWS, WIDTH), b16),
            pltpu.VMEM((WIDTH, 3 * WIDTH), b16),
            pltpu.VMEM((WIDTH, WIDTH), b16),
            dma((4,)),
        ),
        flops=4 * 10**8,
    )(active[0], values, cot, gains, w_qkv, w_out)

    parity = position % 2
    slabs = jnp.stack([position, position + 1 - 2 * parity, position - 1 + 2 * parity])
    ids = (slabs[:, None] * SIDE + jnp.arange(SIDE)[None, :]).reshape(-1)
    seen = jnp.any((lists[:, :, None] == ids) & (lists[:, :, None] >= 0), axis=1)
    hidden = jnp.where(seen, 0.0, HIDDEN).T.astype(b16)
    fk = jnp.repeat(hidden, block, axis=0)
    fk = jnp.pad(fk, ((0, KEYS - 3 * ROWS), (0, 0)), constant_values=HIDDEN)
    fk = jnp.pad(fk, ((0, 0), (0, 128 - SIDE)))
    row_block = lax.broadcasted_iota(jnp.int32, (ROWS, 128), 0) // block
    fq = (row_block == lax.broadcasted_iota(jnp.int32, (ROWS, 128), 1)).astype(b16)

    pair_rows = (HEADS // 2, 2 * ROWS, KEYS)
    send, d_table, d_queries, normed_t, attn_t = local(
        attention_kernel,
        "attention",
        (half_rows, ((2 * WIDTH, KEYS), b16), rows, ((WIDTH, KEYS), b16), ((WIDTH, ROWS), b16)),
        [scalar] + [whole] * 12,
        32,
        (
            pltpu.VMEM((KEYS, WIDTH), b16),
            pltpu.VMEM((KEYS, 2 * WIDTH), b16),
            pltpu.VMEM(pair_rows, f32),
            pltpu.VMEM(pair_rows, b16),
            pltpu.VMEM(pair_rows, f32),
            pltpu.VMEM(pair_rows, b16),
        ),
        flops=3 * 10**9,
        moved=4 * 10**6,
    )(core, near, far, own, kv, q8, q8t, g, scaled, fq, fk, gains, w_qkv)

    pair = [(0, 1), (1, 0)]
    arrived = lax.ppermute(send, "c", pair)
    held, base, back_near, back_far = local(
        back_kernel,
        "back",
        (half_rows, ((ROWS, WIDTH), f32), rows, rows),
        [scalar] + [whole] * 6,
        8,
        flops=10**9,
    )(core, d_table, d_queries, normed_t, attn_t, scaled, w_qkv)
    half = (held.astype(f32) + arrived.astype(f32)).astype(b16)
    half, base, back_near, back_far = lax.optimization_barrier((half, base, back_near, back_far))
    back_near = swapped(back_near, 0)
    count = lax.axis_size(SPACE)
    middle = count // 2
    moved = lax.ppermute(back_far, SPACE, [(middle - 1, 0), (middle, count - 1)])
    plane, ring = len(PLANES[0]), len(RINGS[0])
    parts = half.reshape(plane, 2 * WIDTH // plane, WIDTH)
    part = total(exchanged(parts, PLANES))
    moved, back_near = lax.optimization_barrier((moved, back_near))
    at_end = jnp.logical_or(position == 0, position == count - 1)
    pairs = [(i, i + 1) for i in range(1, count - 1, 2) if i != middle - 1]
    pairs = pairs + [(b, a) for a, b in pairs] + [(0, middle), (count - 1, middle - 1)]
    back_far = lax.ppermute(jnp.where(at_end, moved, back_far), SPACE, pairs)
    parts = exchanged(jnp.broadcast_to(part[None], (ring,) + part.shape), RINGS)
    (copies,) = local(gather_kernel, "gather", (((plane,) + part.shape, b16),), [whole], 4)(parts)
    half = exchanged(copies, PLANES).reshape(2 * WIDTH, WIDTH)
    (grad_input,) = local(input_kernel, "grad_input", (rows,), [whole] * 6, 8, flops=10**10)(
        base, back_near, back_far, values, cot, gains
    )
    half, grad_input = lax.optimization_barrier((half, grad_input))
    other = lax.ppermute(half, "c", pair)

    grad_wqkv, grad_wout, grad_gain = local(
        output_kernel,
        "outputs",
        (((WIDTH, 3 * WIDTH), f32), ((WIDTH, WIDTH), f32), ((WIDTH,), f32)),
        [scalar] + [whole] * 4,
        8,
        moved=4 * 10**6,
    )(core, half, other, w_qkv, gain)
    return (grad_input[None], grad_wqkv, grad_wout, grad_gain)


def solution(mesh):
    fine = Mesh(mesh.devices.reshape(SIZES), AXES)
    region = ("yl", "c")
    split = P(region, SPACE, None)
    return jax.shard_map(
        shards,
        mesh=fine,
        in_specs=(split, split, split, P(region, SPACE), P(), P(), P()),
        out_specs=(split, P(), P(), P()),
        check_vma=False,
    )
```

```python
import math

import jax
import jax.numpy as jnp
import numpy as np
from jax import lax
from jax.experimental import pallas as pl
from jax.experimental.pallas import tpu as pltpu
from jax.sharding import Mesh
from jax.sharding import PartitionSpec as P

HEADS = 6
SIDE = 9
ROWS = 288
WIDTH = 384
HEAD = 64
KEYS = 896
SPACE = ("yh", "x", "z")
HIDDEN = -1e30


def inner(left, right):
    return lax.dot_general(
        left, right, (((1,), (1,)), ((), ())), preferred_element_type=jnp.float32
    )


def dot(left, right):
    return jnp.dot(left, right, preferred_element_type=jnp.float32)


def swapped(block, first):
    count = lax.axis_size(SPACE)
    pairs = [(i, i + 1) for i in range(first, count - 1, 2)]
    return lax.ppermute(block, SPACE, pairs + [(b, a) for a, b in pairs])


AXES = ("yl", "c", "yh", "x", "z")
SIZES = (4, 2, 2, 4, 8)
GRID = np.arange(math.prod(SIZES)).reshape(SIZES)
PLANES = [GRID[i, 0, j].ravel().tolist() for i in range(4) for j in range(2)]
PLANES += [GRID[:, 1, :, :, k].ravel().tolist() for k in range(8)]
RINGS = [GRID[:, 0, :, i, k].ravel().tolist() for i in range(4) for k in range(8)]
RINGS += [GRID[i, 1, j, k].ravel().tolist() for i in range(4) for j in range(2) for k in range(4)]


def exchanged(parts, groups):
    return lax.all_to_all(parts, AXES, 0, 0, axis_index_groups=groups, tiled=True)


def total(parts):
    return jnp.sum(parts.astype(jnp.float32), axis=0).astype(jnp.bfloat16)


def unit_rows(values, gain):
    power = jnp.mean(values * values, axis=1, keepdims=True)
    return values * lax.rsqrt(power + 1e-06) * gain


def fetch(pairs, sems):
    copies = [
        pltpu.make_async_copy(source, target, sems.at[i]) for i, (source, target) in enumerate(pairs)
    ]
    for copy in copies:
        copy.start()
    return copies


def prepare_kernel(
    alive, tokens_in, cot_in, gain, wqkv_in, wout_in, own, kv, q8, q8t, g, scaled,
    tokens, cot, wqkv, wout, sems,
):
    copies = fetch([(tokens_in, tokens), (wqkv_in, wqkv), (cot_in, cot), (wout_in, wout)], sems)
    copies[0].wait()
    own[...] = unit_rows(tokens[...].astype(jnp.float32), gain[...]).astype(jnp.bfloat16)
    copies[1].wait()
    queries = dot(own[...], wqkv[:, 0:WIDTH]).astype(jnp.bfloat16).astype(jnp.float32)
    eighth = (queries * (1.0 / math.sqrt(HEAD))).astype(jnp.bfloat16)
    q8[...] = eighth
    q8t[...] = eighth.T
    kv[...] = dot(own[...], wqkv[:, WIDTH:]).astype(jnp.bfloat16)
    copies[2].wait()
    block = ROWS // SIDE
    for at in range(SIDE):
        rows = slice(at * block, at * block + block)
        part = cot[rows].astype(jnp.float32) * alive[at].astype(jnp.float32)
        scaled[rows] = part.astype(jnp.bfloat16)
    copies[3].wait()
    g[...] = inner(scaled[...], wout[...]).astype(jnp.bfloat16)


def attention_kernel(
    core, near, far, own, kv, q8, q8t, g, scaled, fq, fk, gain, wqkv,
    send, dt, dq, normed_t, attn_t, normed, table, scores, expo, dshare, dscores,
):
    normed[0:ROWS] = own[...]
    normed[3 * ROWS : KEYS] = jnp.zeros((KEYS - 3 * ROWS, WIDTH), jnp.bfloat16)
    table[0:ROWS] = kv[...]
    table[3 * ROWS : KEYS] = jnp.zeros((KEYS - 3 * ROWS, 2 * WIDTH), jnp.bfloat16)
    for side, halo in enumerate((near, far)):
        rows = slice((side + 1) * ROWS, (side + 2) * ROWS)
        unit = unit_rows(halo[...].astype(jnp.float32), gain[...]).astype(jnp.bfloat16)
        normed[rows] = unit
        table[rows] = dot(unit, wqkv[:, WIDTH:]).astype(jnp.bfloat16)
    normed_t[...] = normed[...].T
    both = lax.broadcasted_iota(jnp.int32, (2 * ROWS, 128), 0) < ROWS
    low = lax.broadcasted_iota(jnp.int32, (2 * ROWS, 128), 1) < HEAD
    keep = both == low
    zero = jnp.zeros((2 * ROWS, 128), jnp.float32)
    chunks = [slice(at, at + 32) for at in range(0, 2 * ROWS, 32)]
    pairs = range(HEADS // 2)
    lanes = [slice(pair * 128, pair * 128 + 128) for pair in pairs]
    values = [slice(WIDTH + at.start, WIDTH + at.stop) for at in lanes]
    shares, results, grads, deltas = [], [], [], []

    def twice(block):
        return jnp.concatenate([block, block], axis=0).astype(jnp.float32)

    def joined(block):
        return jnp.where(low[:ROWS], block[:ROWS], block[ROWS:]).astype(jnp.bfloat16)

    for pair in pairs:
        queries = jnp.where(keep, twice(q8[:, lanes[pair]]), zero).astype(jnp.bfloat16)
        queries = jnp.concatenate([queries, jnp.concatenate([fq[...], fq[...]], axis=0)], axis=1)
        scores[pair] = inner(queries, jnp.concatenate([table[:, lanes[pair]], fk[...]], axis=1))
    for pair in pairs:
        share = []
        for rows in chunks:
            block = scores[pair, rows]
            block = jnp.exp(block - jnp.max(block, axis=1, keepdims=True))
            share.append(1.0 / jnp.sum(block, axis=1, keepdims=True))
            expo[pair, rows] = block.astype(jnp.bfloat16)
        shares.append(jnp.concatenate(share, axis=0))
        results.append(dot(expo[pair], table[:, values[pair]]) * shares[pair])
        grad = jnp.where(keep, twice(g[:, lanes[pair]]) * shares[pair], zero)
        grads.append(grad.astype(jnp.bfloat16))
        dshare[pair] = inner(grads[pair], table[:, values[pair]])
        delta = grads[pair].astype(jnp.float32) * results[pair]
        deltas.append(jnp.sum(delta, axis=1, keepdims=True))
    for pair in pairs:
        for rows in chunks:
                block = (dshare[pair, rows] - deltas[pair][rows]).astype(jnp.bfloat16)
                dscores[pair, rows] = expo[pair, rows] * block
    for pair in pairs:
        moved = dot(dscores[pair], table[:, lanes[pair]]) * (1.0 / math.sqrt(HEAD))
        dq[:, lanes[pair]] = joined(moved)
        attn_t[lanes[pair]] = joined(results[pair]).T
        turned = (grads[pair][:ROWS] + grads[pair][ROWS:]).T
        for half in range(2):
            rows = slice(half * ROWS, half * ROWS + ROWS)
            at = (2 * pair + half) * HEAD
            part = q8t[at : at + HEAD]
            dt[at : at + HEAD] = dot(part, dscores[pair, rows]).astype(jnp.bfloat16)
            part = turned[half * HEAD : half * HEAD + HEAD]
            at += WIDTH
            dt[at : at + HEAD] = dot(part, expo[pair, rows]).astype(jnp.bfloat16)

    @pl.when(core[0] == 0)
    def _():
        value_half(send, normed_t, dt, attn_t, scaled)

    @pl.when(core[0] == 1)
    def _():
        key_half(send, normed_t, dt, dq)


def key_half(out, normed_t, dt, dq):
    out[0:WIDTH] = dot(normed_t[:, 0:ROWS], dq[...]).astype(jnp.bfloat16)
    out[WIDTH:] = inner(normed_t[...], dt[0:WIDTH]).astype(jnp.bfloat16)


def value_half(out, normed_t, dt, attn_t, scaled):
    out[0:WIDTH] = inner(normed_t[...], dt[WIDTH:]).astype(jnp.bfloat16)
    out[WIDTH:] = dot(attn_t[...], scaled[...]).astype(jnp.bfloat16)


def back_kernel(core, dt, dq, normed_t, attn_t, scaled, wqkv, held, base, near, far):
    back = lax.dot_general(
        dt[...], wqkv[:, WIDTH:], (((0,), (1,)), ((), ())), preferred_element_type=jnp.float32
    )
    near[...] = back[ROWS : 2 * ROWS].astype(jnp.bfloat16)
    far[...] = back[2 * ROWS : 3 * ROWS].astype(jnp.bfloat16)
    base[...] = back[0:ROWS] + inner(dq[...], wqkv[:, 0:WIDTH])

    @pl.when(core[0] == 0)
    def _():
        key_half(held, normed_t, dt, dq)

    @pl.when(core[0] == 1)
    def _():
        value_half(held, normed_t, dt, attn_t, scaled)


def gather_kernel(parts, copies):
    part = jnp.sum(parts[...].astype(jnp.float32), axis=0).astype(jnp.bfloat16)
    copies[...] = jnp.broadcast_to(part[None], copies.shape)


def input_kernel(base, near, far, tokens, cot, gain, grad_input):
    d_normed = base[...] + near[...].astype(jnp.float32) + far[...].astype(jnp.float32)
    inward = d_normed.astype(jnp.bfloat16).astype(jnp.float32) * gain[...]
    values = tokens[...].astype(jnp.float32)
    root = lax.rsqrt(jnp.mean(values * values, axis=1, keepdims=True) + 1e-06)
    slope = jnp.mean(inward * values, axis=1, keepdims=True) * root * root
    moved = cot[...].astype(jnp.float32) + root * (inward - values * slope)
    grad_input[...] = moved.astype(jnp.bfloat16)


def output_kernel(core, mine, other, wqkv, gain, grad_qkv, grad_out, grad_gain):
    scale = 1.0 / math.sqrt(512 * ROWS)
    me = core[0]

    def halves(first, second):
        query = first[0:WIDTH].astype(jnp.float32) * scale
        key = first[WIDTH:].astype(jnp.float32) * scale
        value = second[0:WIDTH].astype(jnp.float32) * scale
        grad_qkv[:, 0:WIDTH] = query
        grad_qkv[:, WIDTH : 2 * WIDTH] = key
        grad_qkv[:, 2 * WIDTH :] = value
        grad_out[...] = second[WIDTH:].astype(jnp.float32) * scale
        moved = query * wqkv[:, 0:WIDTH].astype(jnp.float32)
        moved += key * wqkv[:, WIDTH : 2 * WIDTH].astype(jnp.float32)
        moved += value * wqkv[:, 2 * WIDTH :].astype(jnp.float32)
        grad_gain[...] = jnp.sum(moved.T, axis=0) / gain[...]

    @pl.when(me == 0)
    def _():
        halves(mine, other)

    @pl.when(me == 1)
    def _():
        halves(other, mine)


def local(body, name, shapes, in_specs, vmem, scratch=(), flops=10**8, moved=10**6):
    return pl.pallas_call(
        body,
        out_shape=tuple(jax.ShapeDtypeStruct(shape, kind) for shape, kind in shapes),
        in_specs=in_specs,
        out_specs=(pl.BlockSpec(memory_space=pltpu.VMEM),) * len(shapes),
        scratch_shapes=scratch,
        compiler_params=pltpu.CompilerParams(vmem_limit_bytes=vmem * 2**20),
        cost_estimate=pl.CostEstimate(flops=flops, bytes_accessed=moved, transcendentals=0),
        name=name,
    )


def shards(tokens, cotangent, neighbours, active, gain, w_qkv, w_out):
    values = tokens[0]
    cot = cotangent[0]
    lists = neighbours[0]
    block = ROWS // SIDE
    position = lax.axis_index(SPACE)
    core = jnp.reshape(lax.axis_index("c"), (1,)).astype(jnp.int32)
    near = swapped(values, 0)
    far = swapped(values, 1)
    gains = gain[None]

    b16, f32 = jnp.bfloat16, jnp.float32
    whole = pl.BlockSpec(memory_space=pltpu.VMEM)
    scalar = pl.BlockSpec(memory_space=pltpu.SMEM)
    outside = pl.BlockSpec(memory_space=pltpu.HBM)
    rows = ((ROWS, WIDTH), b16)
    half_rows = ((2 * WIDTH, WIDTH), b16)
    dma = pltpu.SemaphoreType.DMA
    own, kv, q8, q8t, g, scaled = local(
        prepare_kernel,
        "prepare",
        (rows, ((ROWS, 2 * WIDTH), b16), rows, ((WIDTH, ROWS), b16), rows, rows),
        [scalar, outside, outside, whole, outside, outside],
        8,
        (
            pltpu.VMEM((ROWS, WIDTH), b16),
            pltpu.VMEM((ROWS, WIDTH), b16),
            pltpu.VMEM((WIDTH, 3 * WIDTH), b16),
            pltpu.VMEM((WIDTH, WIDTH), b16),
            dma((4,)),
        ),
        flops=4 * 10**8,
    )(active[0], values, cot, gains, w_qkv, w_out)

    parity = position % 2
    slabs = jnp.stack([position, position + 1 - 2 * parity, position - 1 + 2 * parity])
    ids = (slabs[:, None] * SIDE + jnp.arange(SIDE)[None, :]).reshape(-1)
    seen = jnp.any((lists[:, :, None] == ids) & (lists[:, :, None] >= 0), axis=1)
    hidden = jnp.where(seen, 0.0, HIDDEN).T.astype(b16)
    fk = jnp.repeat(hidden, block, axis=0)
    fk = jnp.pad(fk, ((0, KEYS - 3 * ROWS), (0, 0)), constant_values=HIDDEN)
    fk = jnp.pad(fk, ((0, 0), (0, 128 - SIDE)))
    row_block = lax.broadcasted_iota(jnp.int32, (ROWS, 128), 0) // block
    fq = (row_block == lax.broadcasted_iota(jnp.int32, (ROWS, 128), 1)).astype(b16)

    pair_rows = (HEADS // 2, 2 * ROWS, KEYS)
    send, d_table, d_queries, normed_t, attn_t = local(
        attention_kernel,
        "attention",
        (half_rows, ((2 * WIDTH, KEYS), b16), rows, ((WIDTH, KEYS), b16), ((WIDTH, ROWS), b16)),
        [scalar] + [whole] * 12,
        32,
        (
            pltpu.VMEM((KEYS, WIDTH), b16),
            pltpu.VMEM((KEYS, 2 * WIDTH), b16),
            pltpu.VMEM(pair_rows, f32),
            pltpu.VMEM(pair_rows, b16),
            pltpu.VMEM(pair_rows, f32),
            pltpu.VMEM(pair_rows, b16),
        ),
        flops=3 * 10**9,
        moved=4 * 10**6,
    )(core, near, far, own, kv, q8, q8t, g, scaled, fq, fk, gains, w_qkv)

    pair = [(0, 1), (1, 0)]
    arrived = lax.ppermute(send, "c", pair)
    held, base, back_near, back_far = local(
        back_kernel,
        "back",
        (half_rows, ((ROWS, WIDTH), f32), rows, rows),
        [scalar] + [whole] * 6,
        8,
        flops=10**9,
    )(core, d_table, d_queries, normed_t, attn_t, scaled, w_qkv)
    half = (held.astype(f32) + arrived.astype(f32)).astype(b16)
    half, base, back_near, back_far = lax.optimization_barrier((half, base, back_near, back_far))
    back_near = swapped(back_near, 0)
    count = lax.axis_size(SPACE)
    middle = count // 2
    moved = lax.ppermute(back_far, SPACE, [(middle - 1, 0), (middle, count - 1)])
    plane, ring = len(PLANES[0]), len(RINGS[0])
    parts = half.reshape(plane, 2 * WIDTH // plane, WIDTH)
    part = total(exchanged(parts, PLANES))
    at_end = jnp.logical_or(position == 0, position == count - 1)
    pairs = [(i, i + 1) for i in range(1, count - 1, 2) if i != middle - 1]
    pairs = pairs + [(b, a) for a, b in pairs] + [(0, middle), (count - 1, middle - 1)]
    back_far = lax.ppermute(jnp.where(at_end, moved, back_far), SPACE, pairs)
    parts = exchanged(jnp.broadcast_to(part[None], (ring,) + part.shape), RINGS)
    (copies,) = local(gather_kernel, "gather", (((plane,) + part.shape, b16),), [whole], 4)(parts)
    half = exchanged(copies, PLANES).reshape(2 * WIDTH, WIDTH)
    (grad_input,) = local(input_kernel, "grad_input", (rows,), [whole] * 6, 8, flops=10**10)(
        base, back_near, back_far, values, cot, gains
    )
    half, grad_input = lax.optimization_barrier((half, grad_input))
    other = lax.ppermute(half, "c", pair)

    grad_wqkv, grad_wout, grad_gain = local(
        output_kernel,
        "outputs",
        (((WIDTH, 3 * WIDTH), f32), ((WIDTH, WIDTH), f32), ((WIDTH,), f32)),
        [scalar] + [whole] * 4,
        8,
        moved=4 * 10**6,
    )(core, half, other, w_qkv, gain)
    return (grad_input[None], grad_wqkv, grad_wout, grad_gain)


def solution(mesh):
    fine = Mesh(mesh.devices.reshape(SIZES), AXES)
    region = ("yl", "c")
    split = P(region, SPACE, None)
    return jax.shard_map(
        shards,
        mesh=fine,
        in_specs=(split, split, split, P(region, SPACE), P(), P(), P()),
        out_specs=(split, P(), P(), P()),
        check_vma=False,
    )
```
